256 devices in a mesh: wide: 64 (over z, x, core), narrow: 4 (over y).
Axes of the slice: x: 4, y: 4, z: 8, core: 2. Of those that a mesh axis runs over, the one named last changes fastest.
Arguments:
- b_tensor: bfloat16 [4, 4096, 4096], P('narrow', 'wide'), may hold values from -6 to 6
- pair_mask: int32 [4, 64, 64], P('narrow', 'wide'), may hold values 0 or 1
- first_map: int32 [64], replicated, may hold values from 0 to 63, each once
- second_map: int32 [64], replicated, may hold values from 0 to 63, each once
- occ_blocks: bfloat16 [64, 8, 64, 64], P('wide', 'narrow'), may hold values from -0.25 to 0.25
- occ_index: int32 [64, 8], replicated, may hold values from 0 to 63, as said below
- virt_blocks: bfloat16 [64, 8, 64, 64], P('wide', 'narrow'), may hold values from -0.25 to 0.25
- virt_index: int32 [64, 8], replicated, may hold values from 0 to 63, as said below
Outputs:
- result: bfloat16 [4, 4096, 4096], P('narrow', 'wide')
The draws below stay inside these ranges and needn't reach their ends.
Inputs may be any that keep to these rules, and one draw needn't show every extreme that they name: `occ_index`: row a lists 8 different molecules, the first of them a itself. `virt_index`: row c lists 8 different molecules, the first of them c itself.
All inputs are finite; a program needn't handle non-finite values. No bound on the sum of `pair_mask` on one device may be relied on, other than what follows from the above.
Results may differ from the reference program's by a relative error of at most 0.005.
Values may be sent and summed in bfloat16 or wider, within the bound.
No kernel may reach another device: no remote copies, remote signals or barrier semaphores. Data moves between devices by JAX's collectives and lax.ppermute only.
A program may use at most 128 MiB of HBM per device.

```python
import jax
import jax.numpy as jnp
from jax import lax

BLOCK = 64
GREEN_BLOCKS = 8
AUX_DEV = 1
MOLECULES = 64
BASIS = 4096
AUX = 4
N_NARROW = 4


def neighbour_lists(key):
    scores = jax.random.randint(key, (MOLECULES, MOLECULES), 0, 2 ** 20)
    column_ids = jnp.arange(MOLECULES, dtype=jnp.int32)[None, :]
    scores = scores * MOLECULES + column_ids
    diagonal = column_ids == jnp.arange(MOLECULES, dtype=jnp.int32)[:, None]
    scores = jnp.where(diagonal, 2 ** 30, scores)
    values, picked = lax.top_k(scores, GREEN_BLOCKS)
    return picked.astype(jnp.int32)


def draw_occ_index(key, part):
    key = jax.random.fold_in(key, 11)
    return neighbour_lists(key)


def draw_virt_index(key, part):
    key = jax.random.fold_in(key, 23)
    return neighbour_lists(key)


def place_ends(array, stream_key, least, high):
    dims = array.shape
    place = [jax.random.randint(jax.random.fold_in(stream_key, axis), (), 0, dims[axis]) for axis in range(len(dims))]
    array = array.at[tuple(place)].set(least)
    longest = dims.index(max(dims))
    place[longest] = (place[longest] + 1) % dims[longest]
    return array.at[tuple(place)].set(high)


def levels(key, extent, split, least, top_value):
    factor_of, own = 1.0, jax.random.fold_in(key, 6)
    for position, shards_of in split:
        steps = jnp.exp(jax.random.uniform(jax.random.fold_in(own, position), (shards_of,), jnp.float32, least / len(split), top_value / len(split)))
        factor_of = factor_of * jnp.repeat(steps, extent[position] // shards_of).reshape([-1 if axis == position else 1 for axis in range(len(extent))])
    return factor_of


def noise(rng, shape, deviation, most, cuts=(), held_as=jnp.bfloat16):
    values = deviation * jax.random.normal(rng, shape, jnp.float32)
    if cuts:
        values = values * levels(rng, shape, cuts, -0.22, 0.18)
    return jnp.clip(values, -most, most).astype(held_as)


def setup_inputs(seed: int = 0) -> dict:
    splits = jax.random.split(jax.random.key(seed), 9)
    return {
        "b_tensor": noise(splits[0], (AUX, BASIS, BASIS), 1.0, 6.0, ((0, 4), (1, 64))),
        "pair_mask": place_ends((jax.random.randint(splits[1], (N_NARROW, MOLECULES, MOLECULES), 0, 4) < 3).astype(jnp.int32), jax.random.fold_in(splits[1], 1), 0, 1),
        "first_map": jax.random.permutation(splits[2], MOLECULES).astype(jnp.int32),
        "second_map": jax.random.permutation(splits[3], MOLECULES).astype(jnp.int32),
        "occ_blocks": noise(splits[4], (MOLECULES, GREEN_BLOCKS, BLOCK, BLOCK), (GREEN_BLOCKS * BLOCK) ** -0.5, 0.25, ((0, 64), (1, 4))),
        "occ_index": draw_occ_index(jax.random.fold_in(splits[8], 71), 0),
        "virt_blocks": noise(splits[6], (MOLECULES, GREEN_BLOCKS, BLOCK, BLOCK), (GREEN_BLOCKS * BLOCK) ** -0.5, 0.25, ((0, 64), (1, 4))),
        "virt_index": draw_virt_index(jax.random.fold_in(splits[8], 71), 0),
    }


def reference(b_tensor, pair_mask, first_map, second_map, occ_blocks, occ_index, virt_blocks, virt_index):
    inverse = jnp.argsort(first_map).astype(jnp.int32)
    virt_slots = jnp.take(inverse, virt_index, axis=0).astype(jnp.int32)
    groups = (jnp.arange(AUX, dtype=jnp.int32) // AUX_DEV).astype(jnp.int32)
    masks = jnp.take(pair_mask, groups, axis=0)
    occ_float = occ_blocks.astype(jnp.float32)
    virt_float = virt_blocks.astype(jnp.float32)

    def per_aux(member):
        aux_plane, mask_rows = member
        weights = jnp.repeat(mask_rows, BLOCK, axis=1).astype(jnp.bfloat16)
        masked = aux_plane.reshape(MOLECULES, BLOCK, BASIS) * weights[:, None, :]
        tensor_four = masked.astype(jnp.float32).reshape(MOLECULES, BLOCK, MOLECULES, BLOCK)

        def occ_one(entry):
            panel, molecule_list = entry
            columns = jnp.take(tensor_four, molecule_list, axis=2)
            return jnp.einsum("snkm,klm->snl", columns, panel)

        first = lax.map(occ_one, (occ_float, occ_index)).astype(jnp.bfloat16)
        first = lax.optimization_barrier(first)
        mapped_one = first.transpose(1, 2, 0, 3).astype(jnp.float32)

        def virt_one(entry):
            panel, slot_list = entry
            columns = jnp.take(mapped_one, slot_list, axis=0)
            return jnp.einsum("knal,knm->alm", columns, panel)

        second = lax.map(virt_one, (virt_float, virt_slots)).astype(jnp.bfloat16)
        arranged = second.transpose(1, 2, 0, 3)
        return jnp.take(arranged, second_map, axis=0).reshape(BASIS, BASIS)

    return lax.map(per_aux, (b_tensor, masks))
```

```python
import functools
import itertools

import jax
import jax.numpy as jnp
from jax import lax
from jax.experimental import pallas as pl
from jax.experimental.pallas import tpu as pltpu
from jax.sharding import PartitionSpec as P

Z, X, CORES, Y = 8, 4, 2, 4
PART = 8


def invert(map_ref, inverse_ref):
    @pl.loop(0, map_ref.shape[0])
    def _(slot):
        inverse_ref[map_ref[slot]] = slot


def swap_halves(tile):
    half = tile.shape[1] // 2
    return jnp.concatenate([tile[:, half:], tile[:, :half]], axis=1)


def occupied_kernel(parts, index_ref, second_ref, own_ref, *refs):
    piece_refs, row_refs = refs[: CORES * Y], refs[CORES * Y : CORES * Y + len(parts)]
    out_ref, dense_ref, rows_ref, inverse_ref = refs[CORES * Y + len(parts) :]
    _, quarter, width = piece_refs[0].shape
    block = width // 2
    x, core, y = own_ref[1], own_ref[2], own_ref[3]
    invert(second_ref, inverse_ref)
    for (off, start), ref in zip(parts, row_refs):
        place = pl.multiple_of((x + off) % X * block + start, 32)
        rows_ref[pl.ds(place, ref.shape[0]), :] = ref[...]
    side_of = lax.broadcasted_iota(jnp.int32, (quarter, width), 1) // block

    @pl.loop(0, Z * X // PART)
    def _(chunk):
        dense_ref[...] = jnp.zeros_like(dense_ref)
        members = list(itertools.product(range(CORES), range(PART)))
        molecules = [
            (chunk * PART + inner) * CORES + (core + core_off) % CORES
            for core_off, inner in members
        ]
        for y_off in range(Y):
            tiles = [
                piece_refs[core_off * Y + y_off][chunk * PART + inner]
                for core_off, inner in members
            ]
            swapped = [swap_halves(tile) for tile in tiles]
            for side in range(2):
                k = 2 * ((y + y_off) % Y) + side
                placed = []
                for row, molecule in enumerate(molecules):
                    index = index_ref[molecule, k]
                    column = pl.multiple_of(index // 2 * width, width)
                    place = (pl.ds(row * quarter, quarter), pl.ds(column, width))
                    value = jnp.where(index % 2 == side, tiles[row], swapped[row])
                    placed.append(
                        (place, jnp.where(side_of == index % 2, value, dense_ref[place]))
                    )
                for place, value in placed:
                    dense_ref[place] = value
        product = lax.dot_general(
            dense_ref[...], rows_ref[...], (((1,), (1,)), ((), ())),
            preferred_element_type=jnp.float32,
        ).astype(jnp.bfloat16)
        for row, molecule in enumerate(molecules):
            out_ref[inverse_ref[molecule]] = product[row * quarter : (row + 1) * quarter]


def virtual_kernel(
    index_ref, first_ref, own_ref, mine_ref, other_ref, rows_ref, out_ref, table_ref, inverse_ref
):
    quarter, width = rows_ref.shape[1], mine_ref.shape[4]
    block = width // 2
    core, y = own_ref[2], own_ref[3]
    z_now = pl.program_id(0)

    @pl.when(z_now == 0)
    def _():
        invert(first_ref, inverse_ref)
        for z, c, high in itertools.product(range(Z), range(CORES), range(2)):
            tile = jnp.concatenate(
                [
                    rows_ref[(z * X + x) * CORES + c, :, high * width : (high + 1) * width]
                    for x in range(X)
                ],
                axis=0,
            )
            place = (z * CORES + c) * 2 + high
            table_ref[place] = tile
            table_ref[Z * CORES * 2 + place] = swap_halves(tile)

    def stored(molecule, k):
        slot = inverse_ref[index_ref[molecule, k]]
        x, c = slot // CORES % X, slot % CORES
        return (slot // (X * CORES) * CORES + c) * 2 + x // 2, x % 2

    left_half = lax.broadcasted_iota(jnp.int32, table_ref.shape[1:], 1) < block
    for x in range(X):
        found = []
        for core_off, panel_ref in enumerate((mine_ref, other_ref)):
            molecule = (z_now * X + x) * CORES + (core + core_off) % CORES
            left = []
            for y_off in range(Y):
                k = 2 * ((y + y_off) % Y)
                (one, odd_one), (two, odd_two) = stored(molecule, k), stored(molecule, k + 1)
                left.append(
                    jnp.where(
                        left_half,
                        table_ref[Z * CORES * 2 * odd_one + one],
                        table_ref[Z * CORES * 2 * (1 - odd_two) + two],
                    )
                )
            right = [panel_ref[x, y_off, 0] for y_off in range(Y)]
            found.append(
                lax.dot_general(
                    jnp.concatenate(left, axis=1), jnp.concatenate(right, axis=1),
                    (((1,), (1,)), ((), ())), preferred_element_type=jnp.float32,
                )
            )
        both = jnp.where(
            core == 0, jnp.concatenate(found, axis=1), jnp.concatenate(found[::-1], axis=1)
        )
        out_ref[:, x * width : (x + 1) * width] = both.astype(jnp.bfloat16)


def occupied(pieces, parts, rows, own, occ_index, second_map):
    molecules = second_map.shape[0]
    _, quarter, width = pieces[0].shape
    basis = rows[0].shape[1]
    smem = pl.BlockSpec(memory_space=pltpu.SMEM)
    vmem = pl.BlockSpec(memory_space=pltpu.VMEM)
    count = X * width // 2
    return pl.pallas_call(
        functools.partial(occupied_kernel, parts),
        out_shape=jax.ShapeDtypeStruct((molecules, quarter, count), jnp.bfloat16),
        in_specs=[smem] * 3 + [vmem] * (len(pieces) + len(rows)),
        out_specs=vmem,
        scratch_shapes=[
            pltpu.VMEM((PART * CORES * quarter, basis), jnp.bfloat16),
            pltpu.VMEM((count, basis), jnp.bfloat16),
            pltpu.SMEM((molecules,), jnp.int32),
        ],
        compiler_params=pltpu.CompilerParams(vmem_limit_bytes=32 * 2**20),
        cost_estimate=pl.CostEstimate(
            flops=2 * molecules * quarter * count * basis, bytes_accessed=2**22, transcendentals=0
        ),
    )(occ_index, second_map, own, *pieces, *rows)


def virtual(mine, other, rows, own, virt_index, first_map):
    molecules = first_map.shape[0]
    block, width = mine.shape[3:]
    panels = pl.BlockSpec((X, Y, 1, block, width), lambda g, *_: (0, 0, g, 0, 0))
    return pl.pallas_call(
        virtual_kernel,
        out_shape=jax.ShapeDtypeStruct((block, molecules * block), jnp.bfloat16),
        grid_spec=pltpu.PrefetchScalarGridSpec(
            num_scalar_prefetch=3,
            grid=(Z,),
            in_specs=[panels, panels, pl.BlockSpec(rows.shape, lambda g, *_: (0, 0, 0))],
            out_specs=pl.BlockSpec((block, X * width), lambda g, *_: (0, g)),
            scratch_shapes=[
                pltpu.VMEM((molecules, block, width), jnp.bfloat16),
                pltpu.SMEM((molecules,), jnp.int32),
            ],
        ),
        compiler_params=pltpu.CompilerParams(
            dimension_semantics=("arbitrary",), vmem_limit_bytes=48 * 2**20
        ),
        cost_estimate=pl.CostEstimate(
            flops=4 * mine.size * block, bytes_accessed=4 * mine.size, transcendentals=0
        ),
    )(virt_index, first_map, own, mine, other, rows)


def wide_index(z, x, core):
    return (z % Z * X + x % X) * CORES + core % CORES


PLANES = [[wide_index(z, x, c) for z in range(Z) for x in range(X)] for c in range(CORES)]
COLUMNS = [[wide_index(z, x, c) for z in range(Z)] for x in range(X) for c in range(CORES)]
ROWS = [[wide_index(z, x, c) for x in range(X)] for z in range(Z) for c in range(CORES)]


def shift(array, axis, by):
    if axis == "y":
        return lax.ppermute(array, "narrow", [((i + by) % Y, i) for i in range(Y)])
    steps = [by if axis == name else 0 for name in ("z", "x", "core")]
    pairs = []
    for place in itertools.product(range(Z), range(X), range(CORES)):
        source = wide_index(*(at + step for at, step in zip(place, steps)))
        pairs.append((source, wide_index(*place)))
    return lax.ppermute(array, "wide", pairs)


def exchange(array, groups):
    return lax.all_to_all(
        array, "wide", split_axis=0, concat_axis=0, tiled=True, axis_index_groups=groups
    )


def ring(array, axis):
    middle = array.shape[0] // 2
    after, before = shift(array, axis, 1), shift(array, axis, -1)
    low, high = shift(before[:middle], axis, -1), shift(after[middle:], axis, 1)
    return [(0, 0, array), (1, 0, after), (2, 0, low), (2, middle, high), (3, 0, before)]


def per_device(
    b_tensor, pair_mask, first_map, second_map, occ_blocks, occ_index, virt_blocks, virt_index
):
    block = b_tensor.shape[1]
    wide, narrow = lax.axis_index("wide"), lax.axis_index("narrow")
    own = [wide // (X * CORES), wide // CORES % X, wide % CORES, narrow]
    own = jnp.stack(own).astype(jnp.int32)
    masked = b_tensor[0] * jnp.repeat(pair_mask[0, 0], block).astype(jnp.bfloat16)[None]
    parts = ring(masked, "x")
    occ_piece = occ_blocks[0].transpose(1, 0, 2).reshape(block, -1)
    virt_piece = virt_blocks[0].transpose(2, 0, 1).reshape(block, -1)
    quarters = exchange(jnp.tile(occ_piece, (Z, 1)), PLANES).reshape(Z * X, block // X, -1)
    mine = [quarters] + [shift(quarters, "y", by) for by in range(1, Y)]
    pieces = mine + [shift(piece, "core", 1) for piece in mine]
    column = exchange(jnp.tile(virt_piece, (Z, 1)), COLUMNS).reshape(Z, *virt_piece.shape)
    plane = jnp.stack([column] + [shift(column, "y", by) for by in range(1, Y)])
    mine = lax.all_gather(plane, "wide", axis=0, axis_index_groups=ROWS)
    other = shift(mine, "core", 1)
    half = occupied(
        pieces, [part[:2] for part in parts], [part[2] for part in parts], own, occ_index,
        second_map,
    )
    rows = lax.all_to_all(half, "wide", split_axis=0, concat_axis=0, tiled=True)
    return virtual(mine, other, rows, own, virt_index, first_map)[None]


def solution(mesh):
    placed = (
        P("narrow", "wide", None),
        P("narrow", "wide", None),
        P(),
        P(),
        P("wide", "narrow", None, None),
        P(),
        P("wide", "narrow", None, None),
        P(),
    )
    return jax.shard_map(
        per_device, mesh=mesh, in_specs=placed, out_specs=P("narrow", "wide", None), check_vma=False
    )
```

```python
import functools
import itertools

import jax
import jax.numpy as jnp
from jax import lax
from jax.experimental import pallas as pl
from jax.experimental.pallas import tpu as pltpu
from jax.sharding import Mesh, PartitionSpec as P

Z, X, CORES, Y = 8, 4, 2, 4
BLOCK, WIDTH, QUARTER = 64, 128, 16
MOLECULES = Z * X * CORES
BASIS = MOLECULES * BLOCK
ANYWHERE = pl.BlockSpec(memory_space=pl.ANY)
SMEM = pl.BlockSpec(memory_space=pltpu.SMEM)
VMEM = pl.BlockSpec(memory_space=pltpu.VMEM)
NT = (((1,), (1,)), ((), ()))


def swap_halves(tile):
    return jnp.concatenate([tile[:, BLOCK:], tile[:, :BLOCK]], axis=1)


def small(kernel, outs, in_specs, scratch=()):
    return pl.pallas_call(
        kernel,
        out_shape=tuple(jax.ShapeDtypeStruct(shape, jnp.bfloat16) for shape in outs),
        in_specs=in_specs,
        out_specs=(VMEM,) * len(outs),
        scratch_shapes=list(scratch),
        compiler_params=pltpu.CompilerParams(vmem_limit_bytes=8 * 2**20),
    )


def fetch(pairs, sems):
    copies = [
        pltpu.make_async_copy(source, target, sems.at[number])
        for number, (source, target) in enumerate(pairs)
    ]
    for copy in copies:
        copy.start()
    for copy in copies:
        copy.wait()


def pieces_kernel(own_ref, occ_hbm, virt_hbm, occ_out, virt_out, occ_ref, virt_ref, turn_ref, sems):
    fetch([(occ_hbm, occ_ref), (virt_hbm, virt_ref)], sems)
    turn_ref[...] = jnp.concatenate([occ_ref[0, 0], occ_ref[0, 1]], axis=1)
    for off in range(X):
        start = pl.multiple_of(((own_ref[1] + off) & (X - 1)) * QUARTER, QUARTER)
        occ_out[off] = turn_ref[pl.ds(start, QUARTER), :]
    rows = jnp.concatenate([virt_ref[0, 0], virt_ref[0, 1]], axis=0).astype(jnp.float32)
    virt_out[...] = rows.T.astype(jnp.bfloat16)


def make_pieces(own, occ_blocks, virt_blocks):
    return small(
        pieces_kernel,
        [(X, QUARTER, WIDTH), (BLOCK, WIDTH)],
        [SMEM, ANYWHERE, ANYWHERE],
        [
            pltpu.VMEM(occ_blocks.shape, jnp.bfloat16),
            pltpu.VMEM(virt_blocks.shape, jnp.bfloat16),
            pltpu.VMEM((BLOCK, WIDTH), jnp.bfloat16),
            pltpu.SemaphoreType.DMA((2,)),
        ],
    )(own, occ_blocks, virt_blocks)


def mask_kernel(mask_ref, one_ref, two_ref, three_ref, b_hbm, masked_ref, b_ref, sems):
    del one_ref, two_ref, three_ref
    fetch([(b_hbm, b_ref)], sems)
    first_half = lax.broadcasted_iota(jnp.int32, (BLOCK, WIDTH), 1) < BLOCK
    for pair in range(MOLECULES // 2):
        weight = jnp.where(first_half, mask_ref[0, 0, 2 * pair], mask_ref[0, 0, 2 * pair + 1])
        place = slice(pair * WIDTH, (pair + 1) * WIDTH)
        masked_ref[:, place] = b_ref[0, :, place] * weight.astype(jnp.float32).astype(jnp.bfloat16)


def mask_rows(pair_mask, b_tensor, after):
    return small(
        mask_kernel,
        [(BLOCK, BASIS)],
        [SMEM] + [ANYWHERE] * 4,
        [pltpu.VMEM(b_tensor.shape, jnp.bfloat16), pltpu.SemaphoreType.DMA((1,))],
    )(pair_mask, *after, b_tensor)[0]


def spread_kernel(occ_ref, one_ref, two_ref, three_ref, virt_ref, after_ref, out_ref):
    del after_ref
    for z in range(Z):
        out_ref[z, 0, 0] = occ_ref[0]
        for off, ref in ((1, one_ref), (2, two_ref), (3, three_ref)):
            out_ref[z, 0, off] = ref[...]
        for part in range(X):
            out_ref[z, 1, part] = virt_ref[part * QUARTER : (part + 1) * QUARTER]


def divide_kernel(both_ref, after_ref, before_ref, occ_ref, virt_ref):
    del after_ref, before_ref
    for x_off in range(X):
        for z in range(Z):
            occ_ref[x_off, z] = both_ref[z, 0, x_off]
            virt_ref[z, x_off * QUARTER : (x_off + 1) * QUARTER] = both_ref[z, 1, x_off]


def stack_kernel(*refs):
    *parts, out_ref = refs
    for y, ref in enumerate(parts):
        out_ref[y] = ref[...]


def tie(array, after):
    return pl.pallas_call(
        lambda array_ref, after_ref, out_ref: None,
        out_shape=jax.ShapeDtypeStruct(array.shape, array.dtype),
        in_specs=[ANYWHERE, ANYWHERE],
        out_specs=ANYWHERE,
        input_output_aliases={0: 0},
        compiler_params=pltpu.CompilerParams(vmem_limit_bytes=56 * 2**20),
    )(array, after)


PARTS = [(0, 0, BLOCK), (1, 0, BLOCK), (3, 0, BLOCK), (2, 0, BLOCK // 2), (2, BLOCK // 2, BLOCK // 2)]
PIECES = list(itertools.product(range(CORES), range(Y)))


def occupied_kernel(index_ref, second_ref, own_ref, *refs):
    piece_refs, refs = refs[: len(PIECES)], refs[len(PIECES) :]
    row_refs, refs = refs[: len(PARTS)], refs[len(PARTS) :]
    out_ref, rows_ref, even_ref, odd_ref, inverse_ref, sems = refs
    x0, core0, y0 = (own_ref[i] for i in range(1, 4))
    copies = []
    for number, ((off, start, count), source) in enumerate(zip(PARTS, row_refs)):
        place = pl.multiple_of(((x0 + off) & (X - 1)) * BLOCK + start, 32)
        target = rows_ref.at[pl.ds(place, count), :]
        copies.append(pltpu.make_async_copy(source, target, sems.at[number]))
        copies[-1].start()

    @pl.loop(0, MOLECULES)
    def _(slot):
        inverse_ref[second_ref[slot]] = slot

    side_of = lax.broadcasted_iota(jnp.int32, (QUARTER, WIDTH), 1) // BLOCK
    members = list(itertools.product(range(CORES), range(Z)))
    for x_off in range(X):
        dense_ref = odd_ref if x_off % 2 else even_ref
        dense_ref[...] = jnp.zeros_like(dense_ref)
        molecules = [
            (z * X + ((x0 + x_off) & (X - 1))) * CORES + ((core0 + core_off) & (CORES - 1))
            for core_off, z in members
        ]
        for y_off in range(Y):
            tiles = [piece_refs[c * Y + y_off][x_off, z] for c, z in members]
            swapped = [swap_halves(tile) for tile in tiles]
            for side in range(2):
                k = (((y0 + y_off) & (Y - 1)) << 1) + side
                placed = []
                for row, molecule in enumerate(molecules):
                    index = index_ref[k, molecule]
                    place = (
                        pl.ds(row * QUARTER, QUARTER),
                        pl.ds(pl.multiple_of((index >> 1) * WIDTH, WIDTH), WIDTH),
                    )
                    parity = index & 1
                    value = jnp.where(parity == side, tiles[row], swapped[row])
                    placed.append((place, jnp.where(side_of == parity, value, dense_ref[place])))
                for place, value in placed:
                    dense_ref[place] = value
        if x_off == 0:
            for copy in copies:
                copy.wait()
        product = lax.dot_general(
            dense_ref[...], rows_ref[...], NT, preferred_element_type=jnp.float32
        ).astype(jnp.bfloat16)
        for row, molecule in enumerate(molecules):
            out_ref[inverse_ref[molecule]] = product[row * QUARTER : (row + 1) * QUARTER]


def occupied(pieces, rows, own, occ_index, second_map):
    dense = (CORES * Z * QUARTER, BASIS)
    return pl.pallas_call(
        occupied_kernel,
        out_shape=jax.ShapeDtypeStruct((MOLECULES, QUARTER, X * BLOCK), jnp.bfloat16),
        in_specs=[SMEM] * 3 + [VMEM] * len(pieces) + [ANYWHERE] * len(rows),
        out_specs=VMEM,
        scratch_shapes=[
            pltpu.VMEM((X * BLOCK, BASIS), jnp.bfloat16),
            pltpu.VMEM(dense, jnp.bfloat16),
            pltpu.VMEM(dense, jnp.bfloat16),
            pltpu.SMEM((MOLECULES,), jnp.int32),
            pltpu.SemaphoreType.DMA((len(rows),)),
        ],
        compiler_params=pltpu.CompilerParams(vmem_limit_bytes=16 * 2**20),
        cost_estimate=pl.CostEstimate(
            flops=2 * X * dense[0] * X * BLOCK * BASIS, bytes_accessed=2**22, transcendentals=0
        ),
    )(occ_index.T, second_map, own, *pieces, *rows)


def table_place(slot):
    z, x, core = slot // (X * CORES), slot // CORES % X, slot % CORES
    return (z * CORES + core) * 2 + x // 2, x % 2


def virtual_kernel(core_off, index_ref, first_ref, own_ref, panel_ref, rows_ref, *refs):
    *before_ref, out_ref, table_ref, left_ref, right_ref = refs
    core0, y0 = own_ref[2], own_ref[3]
    z_now = pl.program_id(0)
    half_table = Z * CORES * 2

    @pl.when(z_now == 0)
    def _():
        for slot in range(MOLECULES):
            place, parity = table_place(slot)
            molecule = first_ref[slot]
            left_ref[molecule] = place + half_table * parity
            right_ref[molecule] = place + half_table * (1 - parity)
        for z, c, high in itertools.product(range(Z), range(CORES), range(2)):
            tile = jnp.concatenate(
                [
                    rows_ref[(z * X + x) * CORES + c, :, high * WIDTH : (high + 1) * WIDTH]
                    for x in range(X)
                ],
                axis=0,
            )
            place = (z * CORES + c) * 2 + high
            table_ref[place] = tile
            table_ref[half_table + place] = swap_halves(tile)

    first_half = lax.broadcasted_iota(jnp.int32, (BLOCK, WIDTH), 1) < BLOCK
    for x in range(X):
        molecule = (z_now * X + x) * CORES + ((core0 + core_off) & (CORES - 1))
        left = []
        for y in range(Y):
            k = ((y0 + y) & (Y - 1)) << 1
            one = left_ref[index_ref[k, molecule]]
            two = right_ref[index_ref[k + 1, molecule]]
            left.append(jnp.where(first_half, table_ref[one], table_ref[two]))
        right = [panel_ref[x, y, 0] for y in range(Y)]
        found = lax.dot_general(
            jnp.concatenate(left, axis=1), jnp.concatenate(right, axis=1), NT,
            preferred_element_type=jnp.float32,
        ).astype(jnp.bfloat16)
        found = jnp.concatenate([found, found], axis=1)
        place = slice(x * WIDTH, (x + 1) * WIDTH)
        if core_off:
            found = jnp.where(first_half == (core0 == 0), before_ref[0][:, place], found)
        out_ref[:, place] = found


def virtual(core_off, panels, rows, own, virt_index, first_map, *before):
    columns = pl.BlockSpec((BLOCK, X * WIDTH), lambda g, *_: (0, g))
    return pl.pallas_call(
        functools.partial(virtual_kernel, core_off),
        out_shape=jax.ShapeDtypeStruct((BLOCK, BASIS), jnp.bfloat16),
        grid_spec=pltpu.PrefetchScalarGridSpec(
            num_scalar_prefetch=3,
            grid=(Z,),
            in_specs=[
                pl.BlockSpec((X, Y, 1, BLOCK, WIDTH), lambda g, *_: (0, 0, g, 0, 0)),
                pl.BlockSpec(rows.shape, lambda g, *_: (0, 0, 0)),
            ]
            + [columns] * len(before),
            out_specs=columns,
            scratch_shapes=[
                pltpu.VMEM((MOLECULES, BLOCK, WIDTH), jnp.bfloat16),
                pltpu.SMEM((MOLECULES,), jnp.int32),
                pltpu.SMEM((MOLECULES,), jnp.int32),
            ],
        ),
        input_output_aliases={5: 0} if before else {},
        compiler_params=pltpu.CompilerParams(
            dimension_semantics=("arbitrary",), vmem_limit_bytes=(16 if before else 56) * 2**20
        ),
        cost_estimate=pl.CostEstimate(
            flops=2 * panels.size * BLOCK, bytes_accessed=2 * panels.size, transcendentals=0
        ),
    )(virt_index.T, first_map, own, panels, rows, *before)


SIZES = {"z": Z, "x": X, "core": CORES, "y": Y}


def shift(array, axis, by):
    size = SIZES[axis]
    return lax.ppermute(array, axis, [((i + by) % size, i) for i in range(size)])


def per_device(
    b_tensor, pair_mask, first_map, second_map, occ_blocks, occ_index, virt_blocks, virt_index
):
    own = jnp.stack([lax.axis_index(axis) for axis in SIZES]).astype(jnp.int32)
    occ_piece, virt_piece = make_pieces(own, occ_blocks, virt_blocks)
    quarters = [shift(occ_piece[X - off], "x", off) for off in range(1, X)]
    masked = mask_rows(pair_mask, b_tensor, quarters)
    after, before = shift(masked, "x", 1), shift(masked, "x", -1)
    middle = BLOCK // 2
    low, high = shift(before[:middle], "x", -1), shift(after[middle:], "x", 1)
    spread = small(spread_kernel, [(Z, 2, X, QUARTER, WIDTH)], [VMEM] * 5 + [ANYWHERE])(
        occ_piece, *quarters, virt_piece, masked
    )[0]
    both = lax.all_to_all(spread, "z", split_axis=0, concat_axis=0, tiled=True)
    occ_column, virt_column = small(
        divide_kernel, [(X, Z, QUARTER, WIDTH), (Z, BLOCK, WIDTH)], [VMEM, ANYWHERE, ANYWHERE]
    )(both, after, before)
    pieces = [occ_column] + [shift(occ_column, "y", by) for by in range(1, Y)]
    pieces = pieces + [shift(part, "core", 1) for part in pieces]
    virt_plane = small(stack_kernel, [(Y, Z, BLOCK, WIDTH)], [VMEM] * Y)(
        virt_column, *[shift(virt_column, "y", by) for by in range(1, Y)]
    )[0]
    mine = lax.all_gather(virt_plane, "x", axis=0)
    half = occupied(pieces, [masked, after, before, low, high], own, occ_index, second_map)
    rows = lax.all_to_all(half, ("z", "x", "core"), split_axis=0, concat_axis=0, tiled=True)
    mine = tie(mine, rows)
    other = shift(mine, "core", 1)
    known = (rows, own, virt_index, first_map)
    return virtual(1, other, *known, virtual(0, mine, *known))[None]


def solution(mesh):
    shaped = Mesh(mesh.devices.reshape(Z, X, CORES, Y), tuple(SIZES))
    wide = ("z", "x", "core")
    placed = (
        P("y", wide, None),
        P("y", wide, None),
        P(),
        P(),
        P(wide, "y", None, None),
        P(),
        P(wide, "y", None, None),
        P(),
    )
    return jax.shard_map(
        per_device, mesh=shaped, in_specs=placed, out_specs=P("y", wide, None), check_vma=False
    )
```

```python
import functools
import itertools

import jax
import jax.numpy as jnp
from jax import lax
from jax.experimental import pallas as pl
from jax.experimental.pallas import tpu as pltpu
from jax.sharding import Mesh, PartitionSpec as P

Z, X, CORES, Y = 8, 4, 2, 4
SIZES = {"z": Z, "x": X, "core": CORES, "y": Y}
CHIPS = Z * X
BLOCK, WIDTH, QUARTER = 64, 128, 16
MOLECULES = CHIPS * CORES
BASIS = MOLECULES * BLOCK
ANYWHERE = pl.BlockSpec(memory_space=pl.ANY)
SMEM = pl.BlockSpec(memory_space=pltpu.SMEM)
VMEM = pl.BlockSpec(memory_space=pltpu.VMEM)
NT = (((1,), (1,)), ((), ()))


def swap_halves(tile):
    return jnp.concatenate([tile[:, BLOCK:], tile[:, :BLOCK]], axis=1)


def call(kernel, outs, in_specs, out_specs, scratch=(), mib=16, flops=2**18, moved=2**20):
    return pl.pallas_call(
        kernel,
        out_shape=tuple(jax.ShapeDtypeStruct(shape, jnp.bfloat16) for shape in outs),
        in_specs=in_specs,
        out_specs=out_specs,
        scratch_shapes=list(scratch),
        compiler_params=pltpu.CompilerParams(vmem_limit_bytes=mib * 2**20),
        cost_estimate=pl.CostEstimate(flops=flops, bytes_accessed=moved, transcendentals=0),
    )


def started(pairs, sems):
    copies = [
        pltpu.make_async_copy(source, target, sems.at[number])
        for number, (source, target) in enumerate(pairs)
    ]
    for copy in copies:
        copy.start()
    return copies


def prepare_kernel(
    mask_ref, b_hbm, occ_hbm, virt_hbm, masked_ref, spread_ref, b_ref, occ_ref, virt_ref, sems
):
    b_copy, *others = started([(b_hbm, b_ref), (occ_hbm, occ_ref), (virt_hbm, virt_ref)], sems)
    for copy in others:
        copy.wait()
    occ = jnp.concatenate([occ_ref[0, 0], occ_ref[0, 1]], axis=1)
    rows = jnp.concatenate([virt_ref[0, 0], virt_ref[0, 1]], axis=0).astype(jnp.float32)
    virt = rows.T.astype(jnp.bfloat16)
    for z, x in itertools.product(range(Z), range(X)):
        spread_ref[z * X + x, :QUARTER] = occ[x * QUARTER : (x + 1) * QUARTER]
        spread_ref[z * X + x, QUARTER:] = virt
    b_copy.wait()
    first_half = lax.broadcasted_iota(jnp.int32, (BLOCK, WIDTH), 1) < BLOCK
    for pair in range(MOLECULES // 2):
        weight = jnp.where(first_half, mask_ref[0, 0, 2 * pair], mask_ref[0, 0, 2 * pair + 1])
        place = slice(pair * WIDTH, (pair + 1) * WIDTH)
        masked_ref[:, place] = b_ref[0, :, place] * weight.astype(jnp.float32).astype(jnp.bfloat16)


def prepare(pair_mask, b_tensor, occ_blocks, virt_blocks):
    arrays = (b_tensor, occ_blocks, virt_blocks)
    return call(
        prepare_kernel,
        [(BLOCK, BASIS), (CHIPS, QUARTER + BLOCK, WIDTH)],
        [SMEM] + [ANYWHERE] * 3,
        (VMEM, VMEM),
        [pltpu.VMEM(array.shape, jnp.bfloat16) for array in arrays]
        + [pltpu.SemaphoreType.DMA((3,))],
    )(pair_mask, *arrays)


def divide_kernel(both_ref, occ_ref, virt_ref):
    for chip in range(CHIPS):
        occ_ref[chip] = both_ref[chip, :QUARTER]
        virt_ref[chip] = both_ref[chip, QUARTER:]


def divide(both):
    return call(
        divide_kernel, [(CHIPS, QUARTER, WIDTH), (CHIPS, BLOCK, WIDTH)], [VMEM], (VMEM, VMEM)
    )(both)


def tie(arrays, after):
    count = len(arrays)
    return pl.pallas_call(
        lambda *refs: None,
        out_shape=tuple(jax.ShapeDtypeStruct(array.shape, array.dtype) for array in arrays),
        in_specs=[ANYWHERE] * (count + 1),
        out_specs=(ANYWHERE,) * count,
        input_output_aliases={number: number for number in range(count)},
        compiler_params=pltpu.CompilerParams(vmem_limit_bytes=2**20),
    )(*arrays, after)


PARTS = [(0, None), (1, None), (3, None), (2, 0), (2, 1)]
MEMBERS = 16


def occupied_kernel(index_ref, second_ref, own_ref, *refs):
    piece_refs, refs = refs[: CORES * Y], refs[CORES * Y :]
    row_refs, refs = refs[: CORES * len(PARTS)], refs[CORES * len(PARTS) :]
    *_, out_ref, piece_ref, rows_ref, even_ref, odd_ref = refs
    x0, core0, y0 = (own_ref[i] for i in range(1, 4))
    for number, ref in enumerate(piece_refs):
        piece_ref[number * CHIPS : (number + 1) * CHIPS] = ref[...]
    for core_off in range(CORES):
        for (off, part), ref in zip(PARTS, row_refs[core_off * len(PARTS) :]):
            block = ((core0 ^ core_off) << 2) + ((x0 + off) & (X - 1))
            place = pl.multiple_of((block << 6) + (part or 0) * (BLOCK // 2), 32)
            rows_ref[pl.ds(place, ref.shape[0]), :] = ref[...]
    side_of = lax.broadcasted_iota(jnp.int32, (QUARTER, WIDTH), 1) // BLOCK
    even_ref[...] = jnp.zeros_like(even_ref)
    odd_ref[...] = jnp.zeros_like(odd_ref)
    for chunk, dense_ref in enumerate((even_ref, odd_ref)):
        molecules = [
            second_ref[(chunk * MEMBERS + member) * CORES + core0] for member in range(MEMBERS)
        ]
        places = [
            (((molecule & 1) ^ core0) << 7) + (molecule >> 1) for molecule in molecules
        ]
        for y_off in range(Y):
            tiles = [piece_ref[place + y_off * CHIPS] for place in places]
            swapped = [swap_halves(tile) for tile in tiles]
            for side in range(2):
                k = (((y0 + y_off) & (Y - 1)) << 1) + side
                placed = []
                for row, molecule in enumerate(molecules):
                    index = index_ref[k, molecule]
                    place = (
                        pl.ds(row * QUARTER, QUARTER),
                        pl.ds(pl.multiple_of((index >> 1) << 7, WIDTH), WIDTH),
                    )
                    parity = index & 1
                    value = jnp.where(parity == side, tiles[row], swapped[row])
                    placed.append((place, jnp.where(side_of == parity, value, dense_ref[place])))
                for place, value in placed:
                    dense_ref[place] = value
        product = lax.dot_general(
            dense_ref[...], rows_ref[...], NT, preferred_element_type=jnp.float32
        ).astype(jnp.bfloat16)
        for row in range(MEMBERS):
            out_ref[chunk * MEMBERS + row] = product[row * QUARTER : (row + 1) * QUARTER]


def occupied(pieces, rows, own, occ_index, second_map, *early):
    dense = (MEMBERS * QUARTER, BASIS)
    lanes = CORES * X * BLOCK
    return call(
        occupied_kernel,
        [(CHIPS, QUARTER, lanes)],
        [SMEM] * 3 + [VMEM] * (len(pieces) + len(rows)) + [ANYWHERE] * len(early),
        (VMEM,),
        [
            pltpu.VMEM((len(pieces) * CHIPS, QUARTER, WIDTH), jnp.bfloat16),
            pltpu.VMEM((lanes, BASIS), jnp.bfloat16),
            pltpu.VMEM(dense, jnp.bfloat16),
            pltpu.VMEM(dense, jnp.bfloat16),
        ],
        mib=24,
        flops=4 * dense[0] * BASIS * lanes,
        moved=2**23,
    )(occ_index.T, second_map, own, *pieces, *rows, *early)[0]


def virtual_kernel(core_off, index_ref, first_ref, own_ref, *refs):
    panel_refs, refs = refs[: len(PARTS)], refs[len(PARTS) :]
    if core_off:
        table_ref, before_ref, out_hbm, out_ref, left_ref, right_ref, out_sems = refs
    else:
        rows_ref, out_ref, table_ref, left_ref, right_ref = refs
    core0, y0 = own_ref[2], own_ref[3]
    half_table = CHIPS * CORES // 2
    for slot in range(MOLECULES):
        z, x, core = slot // (X * CORES), slot // CORES % X, slot % CORES
        place = z * X + core * 2 + x // 2
        molecule = first_ref[slot]
        left_ref[molecule] = place + half_table * (x % 2)
        right_ref[molecule] = place + half_table * (1 - x % 2)
    if not core_off:
        for z, tile_at in itertools.product(range(Z), range(X)):
            lanes = slice(tile_at * WIDTH, (tile_at + 1) * WIDTH)
            tile = jnp.concatenate([rows_ref[z * X + x, :, lanes] for x in range(X)], axis=0)
            table_ref[z * X + tile_at] = tile
            table_ref[half_table + z * X + tile_at] = swap_halves(tile)

    def panel(y_off, chip):
        if y_off == 2:
            return panel_refs[3 + chip // (CHIPS // 2)][chip % (CHIPS // 2)]
        return panel_refs[{0: 0, 1: 1, 3: 2}[y_off]][chip]

    first_half = lax.broadcasted_iota(jnp.int32, (BLOCK, WIDTH), 1) < BLOCK
    written = []
    for z in range(Z):
        for x in range(X):
            molecule = (z * X + x) * CORES + (core0 ^ core_off)
            left = []
            for y in range(Y):
                k = ((y0 + y) & (Y - 1)) << 1
                one = left_ref[index_ref[k, molecule]]
                two = right_ref[index_ref[k + 1, molecule]]
                left.append(jnp.where(first_half, table_ref[one], table_ref[two]))
            right = [panel(y, z * X + x) for y in range(Y)]
            found = lax.dot_general(
                jnp.concatenate(left, axis=1), jnp.concatenate(right, axis=1), NT,
                preferred_element_type=jnp.float32,
            ).astype(jnp.bfloat16)
            found = jnp.concatenate([found, found], axis=1)
            place = slice((z * X + x) * WIDTH, (z * X + x + 1) * WIDTH)
            if core_off:
                found = jnp.where(first_half == (core0 == 0), before_ref[:, place], found)
            out_ref[:, place] = found
        if core_off:
            place = (slice(None), pl.ds(z * X * WIDTH, X * WIDTH))
            written.append(
                pltpu.make_async_copy(out_ref.at[place], out_hbm.at[place], out_sems.at[z])
            )
            written[-1].start()
    for copy in written:
        copy.wait()


def virtual(core_off, panels, own, virt_index, first_map, *rest):
    shape, table = (BLOCK, BASIS), (MOLECULES, BLOCK, WIDTH)
    scratch = [pltpu.SMEM((MOLECULES,), jnp.int32)] * 2
    if core_off:
        scratch = [pltpu.VMEM(shape, jnp.bfloat16), *scratch, pltpu.SemaphoreType.DMA((Z,))]
    return call(
        functools.partial(virtual_kernel, core_off),
        [shape] if core_off else [shape, table],
        [SMEM] * 3 + [VMEM] * (len(panels) + len(rest)),
        (ANYWHERE,) if core_off else (VMEM, VMEM),
        scratch,
        flops=2 * MOLECULES // 2 * BLOCK * BASIS // 8 * BLOCK,
        moved=2**22,
    )(virt_index.T, first_map, own, *panels, *rest)


def shift(array, axis, by):
    size = SIZES[axis]
    return lax.ppermute(array, axis, [((i + by) % size, i) for i in range(size)])


def ring(array, axis):
    after, before = shift(array, axis, 1), shift(array, axis, -1)
    middle = array.shape[0] // 2
    low, high = shift(before[:middle], axis, -1), shift(after[middle:], axis, 1)
    return [array, after, before, low, high]


def exchange(array):
    return lax.all_to_all(array, ("z", "x"), split_axis=0, concat_axis=0, tiled=True)


def per_device(
    b_tensor, pair_mask, first_map, second_map, occ_blocks, occ_index, virt_blocks, virt_index
):
    own = jnp.stack([lax.axis_index(axis) for axis in SIZES]).astype(jnp.int32)
    masked, spread = prepare(pair_mask, b_tensor, occ_blocks, virt_blocks)
    both = exchange(spread)
    rows = ring(masked, "x")
    rows = rows + [shift(part, "core", 1) for part in rows]
    occ_plane, virt_plane = divide(both)
    pieces = [occ_plane] + [shift(occ_plane, "y", by) for by in range(1, Y)]
    pieces = pieces + [shift(piece, "core", 1) for piece in pieces]
    mine = ring(virt_plane, "y")
    half = occupied(pieces, rows, own, occ_index, second_map, *mine[1:3])
    turned = exchange(half)
    mine = tie(mine, turned)
    other = [shift(panel, "core", 1) for panel in mine]
    known = (own, virt_index, first_map)
    columns, table = virtual(0, mine, *known, turned)
    return virtual(1, other, *known, table, columns)[0][None]


def solution(mesh):
    shaped = Mesh(mesh.devices.reshape(Z, X, CORES, Y), tuple(SIZES))
    wide = ("z", "x", "core")
    placed = (
        P("y", wide, None),
        P("y", wide, None),
        P(),
        P(),
        P(wide, "y", None, None),
        P(),
        P(wide, "y", None, None),
        P(),
    )
    return jax.shard_map(
        per_device, mesh=shaped, in_specs=placed, out_specs=P("y", wide, None), check_vma=False
    )
```

```python
import functools
import itertools

import jax
import jax.numpy as jnp
from jax import lax
from jax.experimental import pallas as pl
from jax.experimental.pallas import tpu as pltpu
from jax.sharding import Mesh, PartitionSpec as P

Z, X, CORES, Y = 8, 4, 2, 4
SIZES = {"z": Z, "x": X, "core": CORES, "y": Y}
CHIPS = Z * X
BLOCK, WIDTH, QUARTER = 64, 128, 16
MOLECULES = CHIPS * CORES
BASIS = MOLECULES * BLOCK
ANYWHERE = pl.BlockSpec(memory_space=pl.ANY)
SMEM = pl.BlockSpec(memory_space=pltpu.SMEM)
VMEM = pl.BlockSpec(memory_space=pltpu.VMEM)
NT = (((1,), (1,)), ((), ()))


def swap_halves(tile):
    return jnp.concatenate([tile[:, BLOCK:], tile[:, :BLOCK]], axis=1)


def call(kernel, outs, in_specs, out_specs, scratch=(), mib=16, flops=2**18, moved=2**20):
    return pl.pallas_call(
        kernel,
        out_shape=tuple(jax.ShapeDtypeStruct(shape, jnp.bfloat16) for shape in outs),
        in_specs=in_specs,
        out_specs=out_specs,
        scratch_shapes=list(scratch),
        compiler_params=pltpu.CompilerParams(vmem_limit_bytes=mib * 2**20),
        cost_estimate=pl.CostEstimate(flops=flops, bytes_accessed=moved, transcendentals=0),
    )


def mask_kernel(mask_ref, b_ref, masked_ref):
    first_half = lax.broadcasted_iota(jnp.int32, (BLOCK, WIDTH), 1) < BLOCK
    for pair in range(MOLECULES // 2):
        weight = jnp.where(first_half, mask_ref[0, 0, 2 * pair], mask_ref[0, 0, 2 * pair + 1])
        place = slice(pair * WIDTH, (pair + 1) * WIDTH)
        masked_ref[:, place] = b_ref[0, :, place] * weight.astype(jnp.float32).astype(jnp.bfloat16)


def mask_rows(pair_mask, b_tensor):
    return call(mask_kernel, [(BLOCK, BASIS)], [SMEM, VMEM], (VMEM,), mib=8)(pair_mask, b_tensor)[0]


def spread_kernel(own_ref, occ_ref, virt_ref, spread_ref):
    del own_ref
    occ = jnp.concatenate([occ_ref[0, 0], occ_ref[0, 1]], axis=1)
    rows = jnp.concatenate([virt_ref[0, 0], virt_ref[0, 1]], axis=0).astype(jnp.float32)
    virt = rows.T.astype(jnp.bfloat16)
    for z, x in itertools.product(range(Z), range(X)):
        spread_ref[z * X + x, :QUARTER] = occ[x * QUARTER : (x + 1) * QUARTER]
        spread_ref[z * X + x, QUARTER:] = virt


def spread(own, occ_blocks, virt_blocks):
    return call(
        spread_kernel, [(CHIPS, QUARTER + BLOCK, WIDTH)], [SMEM, VMEM, VMEM], (VMEM,), mib=8
    )(own, occ_blocks, virt_blocks)[0]


def divide_kernel(both_ref, occ_ref, virt_ref):
    for chip in range(CHIPS):
        occ_ref[chip] = both_ref[chip, :QUARTER]
        virt_ref[chip] = both_ref[chip, QUARTER:]


def divide(both):
    return call(
        divide_kernel,
        [(CHIPS, QUARTER, WIDTH), (CHIPS, BLOCK, WIDTH)],
        [VMEM],
        (VMEM, VMEM),
        mib=8,
    )(both)


def tie(arrays, *after):
    count = len(arrays)
    return pl.pallas_call(
        lambda *refs: None,
        out_shape=tuple(jax.ShapeDtypeStruct(array.shape, array.dtype) for array in arrays),
        in_specs=[ANYWHERE] * (count + len(after)),
        out_specs=(ANYWHERE,) * count,
        input_output_aliases={number: number for number in range(count)},
        compiler_params=pltpu.CompilerParams(vmem_limit_bytes=2**20),
    )(*arrays, *after)


PARTS = [(0, None), (1, None), (3, None), (2, 0), (2, 1)]
MEMBERS = 16


def dense_kernel(index_ref, second_ref, own_ref, *refs):
    *piece_refs, dense_ref, piece_ref = refs
    core0, y0 = own_ref[2], own_ref[3]
    for number, ref in enumerate(piece_refs):
        piece_ref[number * CHIPS : (number + 1) * CHIPS] = ref[...]
    side_of = lax.broadcasted_iota(jnp.int32, (QUARTER, WIDTH), 1) // BLOCK
    dense_ref[...] = jnp.zeros_like(dense_ref)
    for chunk in range(0, CHIPS, MEMBERS):
        molecules = [second_ref[(chunk + member) * CORES + core0] for member in range(MEMBERS)]
        places = [(((molecule & 1) ^ core0) << 7) + (molecule >> 1) for molecule in molecules]
        for y_off in range(Y):
            tiles = [piece_ref[place + y_off * CHIPS] for place in places]
            swapped = [swap_halves(tile) for tile in tiles]
            for side in range(2):
                k = (((y0 + y_off) & (Y - 1)) << 1) + side
                placed = []
                for row, molecule in enumerate(molecules, chunk):
                    index = index_ref[k, molecule]
                    place = (
                        pl.ds(row * QUARTER, QUARTER),
                        pl.ds(pl.multiple_of((index >> 1) << 7, WIDTH), WIDTH),
                    )
                    parity = index & 1
                    value = jnp.where(parity == side, tiles[row - chunk], swapped[row - chunk])
                    placed.append((place, jnp.where(side_of == parity, value, dense_ref[place])))
                for place, value in placed:
                    dense_ref[place] = value


def dense_panel(pieces, own, occ_index, second_map):
    shape = (CHIPS * QUARTER, BASIS)
    return call(
        dense_kernel,
        [shape],
        [SMEM] * 3 + [VMEM] * len(pieces),
        (VMEM,),
        [pltpu.VMEM((len(pieces) * CHIPS, QUARTER, WIDTH), jnp.bfloat16)],
        mib=8,
        flops=2**20,
        moved=2**23,
    )(occ_index.T, second_map, own, *pieces)[0]


def occupied_kernel(own_ref, dense_ref, *refs):
    *row_refs, out_ref, rows_ref = refs
    x0, core0 = own_ref[1], own_ref[2]
    for core_off in range(CORES):
        for (off, part), ref in zip(PARTS, row_refs[core_off * len(PARTS) :]):
            block = ((core0 ^ core_off) << 2) + ((x0 + off) & (X - 1))
            place = pl.multiple_of((block << 6) + (part or 0) * (BLOCK // 2), 32)
            rows_ref[pl.ds(place, ref.shape[0]), :] = ref[...]
    product = lax.dot_general(
        dense_ref[...], rows_ref[...], NT, preferred_element_type=jnp.float32
    ).astype(jnp.bfloat16)
    for chip in range(CHIPS):
        out_ref[chip] = product[chip * QUARTER : (chip + 1) * QUARTER]


def occupied(dense, rows, own):
    lanes = CORES * X * BLOCK
    return call(
        occupied_kernel,
        [(CHIPS, QUARTER, lanes)],
        [SMEM] + [VMEM] * (1 + len(rows)),
        (VMEM,),
        [pltpu.VMEM((lanes, BASIS), jnp.bfloat16)],
        flops=2 * dense.size * lanes,
        moved=2**23,
    )(own, dense, *rows)[0]


def virtual_kernel(core_off, index_ref, first_ref, own_ref, *refs):
    panel_refs, refs = refs[: len(PARTS)], refs[len(PARTS) :]
    if core_off:
        table_ref, before_ref, out_hbm, out_ref, left_ref, right_ref, out_sems = refs
    else:
        rows_ref, out_ref, table_ref, left_ref, right_ref = refs
    core0, y0 = own_ref[2], own_ref[3]
    half_table = CHIPS * CORES // 2
    for slot in range(MOLECULES):
        z, x, core = slot // (X * CORES), slot // CORES % X, slot % CORES
        place = z * X + core * 2 + x // 2
        molecule = first_ref[slot]
        left_ref[molecule] = place + half_table * (x % 2)
        right_ref[molecule] = place + half_table * (1 - x % 2)
    if not core_off:
        for z, tile_at in itertools.product(range(Z), range(X)):
            lanes = slice(tile_at * WIDTH, (tile_at + 1) * WIDTH)
            tile = jnp.concatenate([rows_ref[z * X + x, :, lanes] for x in range(X)], axis=0)
            table_ref[z * X + tile_at] = tile
            table_ref[half_table + z * X + tile_at] = swap_halves(tile)

    def panel(y_off, chip):
        if y_off == 2:
            return panel_refs[3 + chip // (CHIPS // 2)][chip % (CHIPS // 2)]
        return panel_refs[{0: 0, 1: 1, 3: 2}[y_off]][chip]

    first_half = lax.broadcasted_iota(jnp.int32, (BLOCK, WIDTH), 1) < BLOCK
    written = []
    for z in range(Z):
        for x in range(X):
            molecule = (z * X + x) * CORES + (core0 ^ core_off)
            left = []
            for y in range(Y):
                k = ((y0 + y) & (Y - 1)) << 1
                one = left_ref[index_ref[k, molecule]]
                two = right_ref[index_ref[k + 1, molecule]]
                left.append(jnp.where(first_half, table_ref[one], table_ref[two]))
            right = [panel(y, z * X + x) for y in range(Y)]
            found = lax.dot_general(
                jnp.concatenate(left, axis=1), jnp.concatenate(right, axis=1), NT,
                preferred_element_type=jnp.float32,
            ).astype(jnp.bfloat16)
            found = jnp.concatenate([found, found], axis=1)
            place = slice((z * X + x) * WIDTH, (z * X + x + 1) * WIDTH)
            if core_off:
                found = jnp.where(first_half == (core0 == 0), before_ref[:, place], found)
            out_ref[:, place] = found
        if core_off:
            place = (slice(None), pl.ds(z * X * WIDTH, X * WIDTH))
            written.append(
                pltpu.make_async_copy(out_ref.at[place], out_hbm.at[place], out_sems.at[z])
            )
            written[-1].start()
    for copy in written:
        copy.wait()


def virtual(core_off, panels, own, virt_index, first_map, *rest):
    shape, table = (BLOCK, BASIS), (MOLECULES, BLOCK, WIDTH)
    scratch = [pltpu.SMEM((MOLECULES,), jnp.int32)] * 2
    if core_off:
        scratch = [pltpu.VMEM(shape, jnp.bfloat16), *scratch, pltpu.SemaphoreType.DMA((Z,))]
    return call(
        functools.partial(virtual_kernel, core_off),
        [shape] if core_off else [shape, table],
        [SMEM] * 3 + [VMEM] * (len(panels) + len(rest)),
        (ANYWHERE,) if core_off else (VMEM, VMEM),
        scratch,
        flops=2 * MOLECULES // 2 * BLOCK * BASIS // 8 * BLOCK,
        moved=2**22,
    )(virt_index.T, first_map, own, *panels, *rest)


def shift(array, axis, by):
    size = SIZES[axis]
    return lax.ppermute(array, axis, [((i + by) % size, i) for i in range(size)])


def ring(array, axis, *between):
    after, before = shift(array, axis, 1), shift(array, axis, -1)
    if between:
        after, before = tie([after, before], *between)
    middle = array.shape[0] // 2
    low, high = shift(before[:middle], axis, -1), shift(after[middle:], axis, 1)
    return [array, after, before, low, high]


def exchange(array):
    return lax.all_to_all(array, ("z", "x"), split_axis=0, concat_axis=0, tiled=True)


def per_device(
    b_tensor, pair_mask, first_map, second_map, occ_blocks, occ_index, virt_blocks, virt_index
):
    own = jnp.stack([lax.axis_index(axis) for axis in SIZES]).astype(jnp.int32)
    both = exchange(spread(own, occ_blocks, virt_blocks))
    occ_plane, virt_plane = divide(both)
    pieces = [occ_plane] + [shift(occ_plane, "y", by) for by in range(1, Y)]
    rows = ring(mask_rows(pair_mask, b_tensor), "x", *pieces[1:])
    rows = rows + [shift(part, "core", 1) for part in rows]
    (virt_plane,) = tie([virt_plane], *pieces[1:])
    pieces = pieces + [shift(piece, "core", 1) for piece in pieces]
    half = occupied(dense_panel(pieces, own, occ_index, second_map), rows, own)
    mine = ring(virt_plane, "y", half)
    turned = exchange(*tie([half], *mine[1:3]))
    mine = tie(mine, turned)
    other = [shift(panel, "core", 1) for panel in mine]
    known = (own, virt_index, first_map)
    columns, table = virtual(0, mine, *known, turned)
    return virtual(1, other, *known, table, columns)[0][None]


def solution(mesh):
    shaped = Mesh(mesh.devices.reshape(Z, X, CORES, Y), tuple(SIZES))
    wide = ("z", "x", "core")
    placed = (
        P("y", wide, None),
        P("y", wide, None),
        P(),
        P(),
        P(wide, "y", None, None),
        P(),
        P(wide, "y", None, None),
        P(),
    )
    return jax.shard_map(
        per_device, mesh=shaped, in_specs=placed, out_specs=P("y", wide, None), check_vma=False
    )
```

```python
import functools
import itertools

import jax
import jax.numpy as jnp
from jax import lax
from jax.experimental import pallas as pl
from jax.experimental.pallas import tpu as pltpu
from jax.sharding import Mesh, PartitionSpec as P

Z, X, CORES, Y = 8, 4, 2, 4
SIZES = {"z": Z, "x": X, "core": CORES, "y": Y}
CHIPS = Z * X
BLOCK, WIDTH, QUARTER = 64, 128, 16
MOLECULES = CHIPS * CORES
BASIS = MOLECULES * BLOCK
ANYWHERE = pl.BlockSpec(memory_space=pl.ANY)
SMEM = pl.BlockSpec(memory_space=pltpu.SMEM)
VMEM = pl.BlockSpec(memory_space=pltpu.VMEM)
NT = (((1,), (1,)), ((), ()))


def swap_halves(tile):
    return jnp.concatenate([tile[:, BLOCK:], tile[:, :BLOCK]], axis=1)


def call(kernel, outs, in_specs, out_specs, scratch=(), mib=16):
    return pl.pallas_call(
        kernel,
        out_shape=tuple(jax.ShapeDtypeStruct(shape, jnp.bfloat16) for shape in outs),
        in_specs=in_specs,
        out_specs=out_specs,
        scratch_shapes=list(scratch),
        compiler_params=pltpu.CompilerParams(vmem_limit_bytes=mib * 2**20),
        cost_estimate=pl.CostEstimate(flops=2**10, bytes_accessed=2**10, transcendentals=0),
    )


def mask_kernel(mask_ref, b_ref, masked_ref):
    first_half = lax.broadcasted_iota(jnp.int32, (BLOCK, WIDTH), 1) < BLOCK
    for pair in range(MOLECULES // 2):
        weight = jnp.where(first_half, mask_ref[0, 0, 2 * pair], mask_ref[0, 0, 2 * pair + 1])
        place = slice(pair * WIDTH, (pair + 1) * WIDTH)
        masked_ref[:, place] = b_ref[0, :, place] * weight.astype(jnp.float32).astype(jnp.bfloat16)


def mask_rows(pair_mask, b_tensor):
    return call(mask_kernel, [(BLOCK, BASIS)], [SMEM, VMEM], (VMEM,), mib=8)(pair_mask, b_tensor)[0]


def spread_occ_kernel(own_ref, occ_ref, spread_ref):
    del own_ref
    occ = jnp.concatenate([occ_ref[0, 0], occ_ref[0, 1]], axis=1)
    for z, x in itertools.product(range(Z), range(X)):
        spread_ref[z * X + x] = occ[x * QUARTER : (x + 1) * QUARTER]


def spread_virt_kernel(virt_ref, after_ref, spread_ref):
    del after_ref
    rows = jnp.concatenate([virt_ref[0, 0], virt_ref[0, 1]], axis=0).astype(jnp.float32)
    virt = rows.T.astype(jnp.bfloat16)
    for chip in range(CHIPS):
        spread_ref[chip] = virt


def spread(kernel, rows, specs, *arrays):
    return call(kernel, [(CHIPS, rows, WIDTH)], specs, (VMEM,), mib=8)(*arrays)[0]


def tie(arrays, *after):
    count = len(arrays)
    return pl.pallas_call(
        lambda *refs: None,
        out_shape=tuple(jax.ShapeDtypeStruct(array.shape, array.dtype) for array in arrays),
        in_specs=[ANYWHERE] * (count + len(after)),
        out_specs=(ANYWHERE,) * count,
        input_output_aliases={number: number for number in range(count)},
        compiler_params=pltpu.CompilerParams(vmem_limit_bytes=2**20),
    )(*arrays, *after)


PARTS = [(0, None), (1, None), (3, None), (2, 0), (2, 1)]
MEMBERS = 16


def dense_kernel(index_ref, second_ref, own_ref, *refs):
    *piece_refs, dense_ref, piece_ref = refs
    core0, y0 = own_ref[2], own_ref[3]
    for number, ref in enumerate(piece_refs):
        piece_ref[number * CHIPS : (number + 1) * CHIPS] = ref[...]
    side_of = lax.broadcasted_iota(jnp.int32, (QUARTER, WIDTH), 1) // BLOCK
    dense_ref[...] = jnp.zeros_like(dense_ref)
    for chunk in range(0, CHIPS, MEMBERS):
        molecules = [second_ref[(chunk + member) * CORES + core0] for member in range(MEMBERS)]
        places = [(((molecule & 1) ^ core0) << 7) + (molecule >> 1) for molecule in molecules]
        for y_off in range(Y):
            tiles = [piece_ref[place + y_off * CHIPS] for place in places]
            swapped = [swap_halves(tile) for tile in tiles]
            for side in range(2):
                k = (((y0 + y_off) & (Y - 1)) << 1) + side
                placed = []
                for row, molecule in enumerate(molecules, chunk):
                    index = index_ref[k, molecule]
                    place = (
                        pl.ds(row * QUARTER, QUARTER),
                        pl.ds(pl.multiple_of((index >> 1) << 7, WIDTH), WIDTH),
                    )
                    parity = index & 1
                    value = jnp.where(parity == side, tiles[row - chunk], swapped[row - chunk])
                    placed.append((place, jnp.where(side_of == parity, value, dense_ref[place])))
                for place, value in placed:
                    dense_ref[place] = value


def dense_panel(pieces, own, occ_index, second_map):
    shape = (CHIPS * QUARTER, BASIS)
    return call(
        dense_kernel,
        [shape],
        [SMEM] * 3 + [VMEM] * len(pieces),
        (VMEM,),
        [pltpu.VMEM((len(pieces) * CHIPS, QUARTER, WIDTH), jnp.bfloat16)],
        mib=8,
    )(occ_index.T, second_map, own, *pieces)[0]


def occupied_kernel(own_ref, dense_ref, *refs):
    *row_refs, out_ref, rows_ref = refs
    x0, core0 = own_ref[1], own_ref[2]
    for core_off in range(CORES):
        for (off, part), ref in zip(PARTS, row_refs[core_off * len(PARTS) :]):
            block = ((core0 ^ core_off) << 2) + ((x0 + off) & (X - 1))
            place = pl.multiple_of((block << 6) + (part or 0) * (BLOCK // 2), 32)
            rows_ref[pl.ds(place, ref.shape[0]), :] = ref[...]
    product = lax.dot_general(
        dense_ref[...], rows_ref[...], NT, preferred_element_type=jnp.float32
    ).astype(jnp.bfloat16)
    for chip in range(CHIPS):
        out_ref[chip] = product[chip * QUARTER : (chip + 1) * QUARTER]


def occupied(dense, rows, own):
    lanes = CORES * X * BLOCK
    return call(
        occupied_kernel,
        [(CHIPS, QUARTER, lanes)],
        [SMEM] + [VMEM] * (1 + len(rows)),
        (VMEM,),
        [pltpu.VMEM((lanes, BASIS), jnp.bfloat16)],
    )(own, dense, *rows)[0]


def virtual_kernel(core_off, index_ref, first_ref, own_ref, *refs):
    panel_refs, refs = refs[: len(PARTS)], refs[len(PARTS) :]
    if core_off:
        table_ref, before_ref, out_hbm, out_ref, left_ref, right_ref, out_sems = refs
    else:
        rows_ref, out_ref, table_ref, left_ref, right_ref = refs
    core0, y0 = own_ref[2], own_ref[3]
    half_table = CHIPS * CORES // 2
    for slot in range(MOLECULES):
        z, x, core = slot // (X * CORES), slot // CORES % X, slot % CORES
        place = z * X + core * 2 + x // 2
        molecule = first_ref[slot]
        left_ref[molecule] = place + half_table * (x % 2)
        right_ref[molecule] = place + half_table * (1 - x % 2)
    if not core_off:
        for z, tile_at in itertools.product(range(Z), range(X)):
            lanes = slice(tile_at * WIDTH, (tile_at + 1) * WIDTH)
            tile = jnp.concatenate([rows_ref[z * X + x, :, lanes] for x in range(X)], axis=0)
            table_ref[z * X + tile_at] = tile
            table_ref[half_table + z * X + tile_at] = swap_halves(tile)

    def panel(y_off, chip):
        if y_off == 2:
            return panel_refs[3 + chip // (CHIPS // 2)][chip % (CHIPS // 2)]
        return panel_refs[{0: 0, 1: 1, 3: 2}[y_off]][chip]

    first_half = lax.broadcasted_iota(jnp.int32, (BLOCK, WIDTH), 1) < BLOCK
    written = []
    for z in range(Z):
        for x in range(X):
            molecule = (z * X + x) * CORES + (core0 ^ core_off)
            left = []
            for y in range(Y):
                k = ((y0 + y) & (Y - 1)) << 1
                one = left_ref[index_ref[k, molecule]]
                two = right_ref[index_ref[k + 1, molecule]]
                left.append(jnp.where(first_half, table_ref[one], table_ref[two]))
            right = [panel(y, z * X + x) for y in range(Y)]
            found = lax.dot_general(
                jnp.concatenate(left, axis=1), jnp.concatenate(right, axis=1), NT,
                preferred_element_type=jnp.float32,
            ).astype(jnp.bfloat16)
            found = jnp.concatenate([found, found], axis=1)
            place = slice((z * X + x) * WIDTH, (z * X + x + 1) * WIDTH)
            if core_off:
                found = jnp.where(first_half == (core0 == 0), before_ref[:, place], found)
            out_ref[:, place] = found
        if core_off:
            place = (slice(None), pl.ds(z * X * WIDTH, X * WIDTH))
            written.append(
                pltpu.make_async_copy(out_ref.at[place], out_hbm.at[place], out_sems.at[z])
            )
            written[-1].start()
    for copy in written:
        copy.wait()


def virtual(core_off, panels, own, virt_index, first_map, *rest):
    shape, table = (BLOCK, BASIS), (MOLECULES, BLOCK, WIDTH)
    scratch = [pltpu.SMEM((MOLECULES,), jnp.int32)] * 2
    if core_off:
        scratch = [pltpu.VMEM(shape, jnp.bfloat16), *scratch, pltpu.SemaphoreType.DMA((Z,))]
    return call(
        functools.partial(virtual_kernel, core_off),
        [shape] if core_off else [shape, table],
        [SMEM] * 3 + [VMEM] * (len(panels) + len(rest)),
        (ANYWHERE,) if core_off else (VMEM, VMEM),
        scratch,
    )(virt_index.T, first_map, own, *panels, *rest)


def shift(array, axis, by):
    size = SIZES[axis]
    return lax.ppermute(array, axis, [((i + by) % size, i) for i in range(size)])


def ring(array, axis, *between):
    after, before = shift(array, axis, 1), shift(array, axis, -1)
    if between:
        after, before = tie([after, before], *between)
    middle = array.shape[0] // 2
    low, high = shift(before[:middle], axis, -1), shift(after[middle:], axis, 1)
    return [array, after, before, low, high]


def exchange(array):
    return lax.all_to_all(array, ("z", "x"), split_axis=0, concat_axis=0, tiled=True)


def per_device(
    b_tensor, pair_mask, first_map, second_map, occ_blocks, occ_index, virt_blocks, virt_index
):
    own = jnp.stack([lax.axis_index(axis) for axis in SIZES]).astype(jnp.int32)
    occ_spread = spread(spread_occ_kernel, QUARTER, [SMEM, VMEM], own, occ_blocks)
    virt_spread = spread(spread_virt_kernel, BLOCK, [VMEM, ANYWHERE], virt_blocks, occ_spread)
    occ_plane, virt_plane = exchange(occ_spread), exchange(virt_spread)
    pieces = [occ_plane] + [shift(occ_plane, "y", by) for by in range(1, Y)]
    rows = ring(mask_rows(pair_mask, b_tensor), "x", *pieces[1:])
    rows = rows + [shift(part, "core", 1) for part in rows]
    (virt_plane,) = tie([virt_plane], *pieces[1:])
    pieces = pieces + [shift(piece, "core", 1) for piece in pieces]
    half = occupied(dense_panel(pieces, own, occ_index, second_map), rows, own)
    mine = ring(virt_plane, "y", half)
    turned = exchange(*tie([half], *mine[1:3]))
    mine = tie(mine, turned)
    other = [shift(panel, "core", 1) for panel in mine]
    known = (own, virt_index, first_map)
    columns, table = virtual(0, mine, *known, turned)
    return virtual(1, other, *known, table, columns)[0][None]


def solution(mesh):
    shaped = Mesh(mesh.devices.reshape(Z, X, CORES, Y), tuple(SIZES))
    wide = ("z", "x", "core")
    placed = (
        P("y", wide, None),
        P("y", wide, None),
        P(),
        P(),
        P(wide, "y", None, None),
        P(),
        P(wide, "y", None, None),
        P(),
    )
    return jax.shard_map(
        per_device, mesh=shaped, in_specs=placed, out_specs=P("y", wide, None), check_vma=False
    )
```

```python
import functools
import itertools

import jax
import jax.numpy as jnp
from jax import lax
from jax.experimental import pallas as pl
from jax.experimental.pallas import tpu as pltpu
from jax.sharding import Mesh, PartitionSpec as P

Z, X, CORES, Y = 8, 4, 2, 4
SIZES = {"z": Z, "x": X, "core": CORES, "y": Y}
CHIPS = Z * X
BLOCK, WIDTH, QUARTER = 64, 128, 16
MOLECULES = CHIPS * CORES
BASIS = MOLECULES * BLOCK
ANYWHERE = pl.BlockSpec(memory_space=pl.ANY)
SMEM = pl.BlockSpec(memory_space=pltpu.SMEM)
VMEM = pl.BlockSpec(memory_space=pltpu.VMEM)
NT = (((1,), (1,)), ((), ()))


def swap_halves(tile):
    return jnp.concatenate([tile[:, BLOCK:], tile[:, :BLOCK]], axis=1)


def call(kernel, outs, in_specs, out_specs, scratch=(), mib=16):
    return pl.pallas_call(
        kernel,
        out_shape=tuple(jax.ShapeDtypeStruct(shape, jnp.bfloat16) for shape in outs),
        in_specs=in_specs,
        out_specs=out_specs,
        scratch_shapes=list(scratch),
        compiler_params=pltpu.CompilerParams(vmem_limit_bytes=mib * 2**20),
        cost_estimate=pl.CostEstimate(flops=2**10, bytes_accessed=2**10, transcendentals=0),
    )


def mask_kernel(mask_ref, b_ref, masked_ref):
    first_half = lax.broadcasted_iota(jnp.int32, (BLOCK, WIDTH), 1) < BLOCK
    for pair in range(MOLECULES // 2):
        weight = jnp.where(first_half, mask_ref[0, 0, 2 * pair], mask_ref[0, 0, 2 * pair + 1])
        place = slice(pair * WIDTH, (pair + 1) * WIDTH)
        masked_ref[:, place] = b_ref[0, :, place] * weight.astype(jnp.float32).astype(jnp.bfloat16)


def mask_rows(pair_mask, b_tensor):
    return call(mask_kernel, [(BLOCK, BASIS)], [SMEM, VMEM], (VMEM,), mib=8)(pair_mask, b_tensor)[0]


def spread_kernel(own_ref, occ_ref, virt_ref, spread_ref):
    del own_ref
    occ = jnp.concatenate([occ_ref[0, 0], occ_ref[0, 1]], axis=1)
    rows = jnp.concatenate([virt_ref[0, 0], virt_ref[0, 1]], axis=0).astype(jnp.float32)
    virt = rows.T.astype(jnp.bfloat16)
    for z, x in itertools.product(range(Z), range(X)):
        spread_ref[z * X + x, :QUARTER] = occ[x * QUARTER : (x + 1) * QUARTER]
        spread_ref[z * X + x, QUARTER:] = virt


def spread(own, occ_blocks, virt_blocks):
    return call(
        spread_kernel, [(CHIPS, QUARTER + BLOCK, WIDTH)], [SMEM, VMEM, VMEM], (VMEM,), mib=8
    )(own, occ_blocks, virt_blocks)[0]


def divide_kernel(both_ref, occ_ref, virt_ref):
    for chip in range(CHIPS):
        occ_ref[chip] = both_ref[chip, :QUARTER]
        virt_ref[chip] = both_ref[chip, QUARTER:]


def divide(both):
    return call(
        divide_kernel,
        [(CHIPS, QUARTER, WIDTH), (CHIPS, BLOCK, WIDTH)],
        [VMEM],
        (VMEM, VMEM),
        mib=8,
    )(both)


def tie(arrays, *after):
    count = len(arrays)
    return pl.pallas_call(
        lambda *refs: None,
        out_shape=tuple(jax.ShapeDtypeStruct(array.shape, array.dtype) for array in arrays),
        in_specs=[ANYWHERE] * (count + len(after)),
        out_specs=(ANYWHERE,) * count,
        input_output_aliases={number: number for number in range(count)},
        compiler_params=pltpu.CompilerParams(vmem_limit_bytes=2**20),
    )(*arrays, *after)


PARTS = [(0, None), (1, None), (3, None), (2, 0), (2, 1)]
MEMBERS = 16


def dense_kernel(index_ref, second_ref, own_ref, *refs):
    *piece_refs, dense_ref, piece_ref = refs
    core0, y0 = own_ref[2], own_ref[3]
    for number, ref in enumerate(piece_refs):
        piece_ref[number * CHIPS : (number + 1) * CHIPS] = ref[...]
    side_of = lax.broadcasted_iota(jnp.int32, (QUARTER, WIDTH), 1) // BLOCK
    dense_ref[...] = jnp.zeros_like(dense_ref)
    for chunk in range(0, CHIPS, MEMBERS):
        molecules = [second_ref[(chunk + member) * CORES + core0] for member in range(MEMBERS)]
        places = [(((molecule & 1) ^ core0) << 7) + (molecule >> 1) for molecule in molecules]
        for y_off in range(Y):
            tiles = [piece_ref[place + y_off * CHIPS] for place in places]
            swapped = [swap_halves(tile) for tile in tiles]
            for side in range(2):
                k = (((y0 + y_off) & (Y - 1)) << 1) + side
                placed = []
                for row, molecule in enumerate(molecules, chunk):
                    index = index_ref[k, molecule]
                    place = (
                        pl.ds(row * QUARTER, QUARTER),
                        pl.ds(pl.multiple_of((index >> 1) << 7, WIDTH), WIDTH),
                    )
                    parity = index & 1
                    value = jnp.where(parity == side, tiles[row - chunk], swapped[row - chunk])
                    placed.append((place, jnp.where(side_of == parity, value, dense_ref[place])))
                for place, value in placed:
                    dense_ref[place] = value


def dense_panel(pieces, own, occ_index, second_map):
    shape = (CHIPS * QUARTER, BASIS)
    return call(
        dense_kernel,
        [shape],
        [SMEM] * 3 + [VMEM] * len(pieces),
        (VMEM,),
        [pltpu.VMEM((len(pieces) * CHIPS, QUARTER, WIDTH), jnp.bfloat16)],
        mib=8,
    )(occ_index.T, second_map, own, *pieces)[0]


def occupied_kernel(own_ref, dense_ref, *refs):
    *row_refs, out_ref, rows_ref = refs
    x0, core0 = own_ref[1], own_ref[2]
    for core_off in range(CORES):
        for (off, part), ref in zip(PARTS, row_refs[core_off * len(PARTS) :]):
            block = ((core0 ^ core_off) << 2) + ((x0 + off) & (X - 1))
            place = pl.multiple_of((block << 6) + (part or 0) * (BLOCK // 2), 32)
            rows_ref[pl.ds(place, ref.shape[0]), :] = ref[...]
    product = lax.dot_general(
        dense_ref[...], rows_ref[...], NT, preferred_element_type=jnp.float32
    ).astype(jnp.bfloat16)
    for chip in range(CHIPS):
        out_ref[chip] = product[chip * QUARTER : (chip + 1) * QUARTER]


def occupied(dense, rows, own):
    lanes = CORES * X * BLOCK
    return call(
        occupied_kernel,
        [(CHIPS, QUARTER, lanes)],
        [SMEM] + [VMEM] * (1 + len(rows)),
        (VMEM,),
        [pltpu.VMEM((lanes, BASIS), jnp.bfloat16)],
    )(own, dense, *rows)[0]


def virtual_kernel(core_off, index_ref, first_ref, own_ref, *refs):
    panel_refs, refs = refs[: len(PARTS)], refs[len(PARTS) :]
    if core_off:
        table_ref, before_ref, out_hbm, out_ref, left_ref, right_ref, out_sems = refs
    else:
        rows_ref, out_ref, table_ref, left_ref, right_ref = refs
    core0, y0 = own_ref[2], own_ref[3]
    half_table = CHIPS * CORES // 2
    for slot in range(MOLECULES):
        z, x, core = slot // (X * CORES), slot // CORES % X, slot % CORES
        place = z * X + core * 2 + x // 2
        molecule = first_ref[slot]
        left_ref[molecule] = place + half_table * (x % 2)
        right_ref[molecule] = place + half_table * (1 - x % 2)
    if not core_off:
        for z, tile_at in itertools.product(range(Z), range(X)):
            lanes = slice(tile_at * WIDTH, (tile_at + 1) * WIDTH)
            tile = jnp.concatenate([rows_ref[z * X + x, :, lanes] for x in range(X)], axis=0)
            table_ref[z * X + tile_at] = tile
            table_ref[half_table + z * X + tile_at] = swap_halves(tile)

    def panel(y_off, chip):
        if y_off == 2:
            return panel_refs[3 + chip // (CHIPS // 2)][chip % (CHIPS // 2)]
        return panel_refs[{0: 0, 1: 1, 3: 2}[y_off]][chip]

    first_half = lax.broadcasted_iota(jnp.int32, (BLOCK, WIDTH), 1) < BLOCK
    written = []
    for z in range(Z):
        for x in range(X):
            molecule = (z * X + x) * CORES + (core0 ^ core_off)
            left = []
            for y in range(Y):
                k = ((y0 + y) & (Y - 1)) << 1
                one = left_ref[index_ref[k, molecule]]
                two = right_ref[index_ref[k + 1, molecule]]
                left.append(jnp.where(first_half, table_ref[one], table_ref[two]))
            right = [panel(y, z * X + x) for y in range(Y)]
            found = lax.dot_general(
                jnp.concatenate(left, axis=1), jnp.concatenate(right, axis=1), NT,
                preferred_element_type=jnp.float32,
            ).astype(jnp.bfloat16)
            found = jnp.concatenate([found, found], axis=1)
            place = slice((z * X + x) * WIDTH, (z * X + x + 1) * WIDTH)
            if core_off:
                found = jnp.where(first_half == (core0 == 0), before_ref[:, place], found)
            out_ref[:, place] = found
        if core_off:
            place = (slice(None), pl.ds(z * X * WIDTH, X * WIDTH))
            written.append(
                pltpu.make_async_copy(out_ref.at[place], out_hbm.at[place], out_sems.at[z])
            )
            written[-1].start()
    for copy in written:
        copy.wait()


def virtual(core_off, panels, own, virt_index, first_map, *rest):
    shape, table = (BLOCK, BASIS), (MOLECULES, BLOCK, WIDTH)
    scratch = [pltpu.SMEM((MOLECULES,), jnp.int32)] * 2
    if core_off:
        scratch = [pltpu.VMEM(shape, jnp.bfloat16), *scratch, pltpu.SemaphoreType.DMA((Z,))]
    return call(
        functools.partial(virtual_kernel, core_off),
        [shape] if core_off else [shape, table],
        [SMEM] * 3 + [VMEM] * (len(panels) + len(rest)),
        (ANYWHERE,) if core_off else (VMEM, VMEM),
        scratch,
    )(virt_index.T, first_map, own, *panels, *rest)


def shift(array, axis, by):
    size = SIZES[axis]
    return lax.ppermute(array, axis, [((i + by) % size, i) for i in range(size)])


def ring(array, axis, *between):
    after, before = shift(array, axis, 1), shift(array, axis, -1)
    if between:
        after, before = tie([after, before], *between)
    middle = array.shape[0] // 2
    low, high = shift(before[:middle], axis, -1), shift(after[middle:], axis, 1)
    return [array, after, before, low, high]


def exchange(array):
    return lax.all_to_all(array, ("z", "x"), split_axis=0, concat_axis=0, tiled=True)


def per_device(
    b_tensor, pair_mask, first_map, second_map, occ_blocks, occ_index, virt_blocks, virt_index
):
    own = jnp.stack([lax.axis_index(axis) for axis in SIZES]).astype(jnp.int32)
    both = exchange(spread(own, occ_blocks, virt_blocks))
    occ_plane, virt_plane = divide(both)
    pieces = [occ_plane] + [shift(occ_plane, "y", by) for by in range(1, Y)]
    rows = ring(mask_rows(pair_mask, b_tensor), "x", occ_plane)
    rows = rows + [shift(part, "core", 1) for part in rows]
    (virt_plane,) = tie([virt_plane], *pieces[1:])
    pieces = pieces + [shift(piece, "core", 1) for piece in pieces]
    half = occupied(dense_panel(pieces, own, occ_index, second_map), rows, own)
    mine = ring(virt_plane, "y", half)
    turned = exchange(*tie([half], *mine[1:3]))
    mine = tie(mine, turned)
    other = [shift(panel, "core", 1) for panel in mine]
    known = (own, virt_index, first_map)
    columns, table = virtual(0, mine, *known, turned)
    return virtual(1, other, *known, table, columns)[0][None]


def solution(mesh):
    shaped = Mesh(mesh.devices.reshape(Z, X, CORES, Y), tuple(SIZES))
    wide = ("z", "x", "core")
    placed = (
        P("y", wide, None),
        P("y", wide, None),
        P(),
        P(),
        P(wide, "y", None, None),
        P(),
        P(wide, "y", None, None),
        P(),
    )
    return jax.shard_map(
        per_device, mesh=shaped, in_specs=placed, out_specs=P("y", wide, None), check_vma=False
    )
```

```python
import functools
import itertools

import jax
import jax.numpy as jnp
from jax import lax
from jax.experimental import pallas as pl
from jax.experimental.pallas import tpu as pltpu
from jax.sharding import Mesh, PartitionSpec as P

Z, X, CORES, Y = 8, 4, 2, 4
SIZES = {"z": Z, "x": X, "core": CORES, "y": Y}
CHIPS = Z * X
HALF = CHIPS // 2
BLOCK, WIDTH, QUARTER = 64, 128, 16
MOLECULES = CHIPS * CORES
BASIS = MOLECULES * BLOCK
ANYWHERE = pl.BlockSpec(memory_space=pl.ANY)
SMEM = pl.BlockSpec(memory_space=pltpu.SMEM)
VMEM = pl.BlockSpec(memory_space=pltpu.VMEM)
NT = (((1,), (1,)), ((), ()))


def swap_halves(tile):
    return jnp.concatenate([tile[:, BLOCK:], tile[:, :BLOCK]], axis=1)


def call(kernel, outs, in_specs, out_specs, scratch=(), mib=16):
    return pl.pallas_call(
        kernel,
        out_shape=tuple(jax.ShapeDtypeStruct(shape, jnp.bfloat16) for shape in outs),
        in_specs=in_specs,
        out_specs=out_specs,
        scratch_shapes=list(scratch),
        compiler_params=pltpu.CompilerParams(vmem_limit_bytes=mib * 2**20),
        cost_estimate=pl.CostEstimate(flops=2**10, bytes_accessed=2**10, transcendentals=0),
    )


def mask_kernel(mask_ref, b_ref, masked_ref):
    first_half = lax.broadcasted_iota(jnp.int32, (BLOCK, WIDTH), 1) < BLOCK
    for pair in range(MOLECULES // 2):
        weight = jnp.where(first_half, mask_ref[0, 0, 2 * pair], mask_ref[0, 0, 2 * pair + 1])
        place = slice(pair * WIDTH, (pair + 1) * WIDTH)
        masked_ref[:, place] = b_ref[0, :, place] * weight.astype(jnp.float32).astype(jnp.bfloat16)


def mask_rows(pair_mask, b_tensor):
    return call(mask_kernel, [(BLOCK, BASIS)], [SMEM, VMEM], (VMEM,), mib=8)(pair_mask, b_tensor)[0]


def spread_kernel(own_ref, occ_ref, virt_ref, spread_ref):
    del own_ref
    occ = jnp.concatenate([occ_ref[0, 0], occ_ref[0, 1]], axis=1)
    rows = jnp.concatenate([virt_ref[0, 0], virt_ref[0, 1]], axis=0).astype(jnp.float32)
    virt = rows.T.astype(jnp.bfloat16)
    for z, x in itertools.product(range(Z), range(X)):
        spread_ref[z * X + x, :QUARTER] = occ[x * QUARTER : (x + 1) * QUARTER]
        spread_ref[z * X + x, QUARTER:] = virt


def spread(own, occ_blocks, virt_blocks):
    return call(
        spread_kernel, [(CHIPS, QUARTER + BLOCK, WIDTH)], [SMEM, VMEM, VMEM], (VMEM,), mib=8
    )(own, occ_blocks, virt_blocks)[0]


def divide_kernel(both_ref, occ_ref, *virt_refs):
    for chip in range(CHIPS):
        occ_ref[chip] = both_ref[chip, :QUARTER]
        virt_refs[chip // HALF][chip % HALF] = both_ref[chip, QUARTER:]


def divide(both):
    return call(
        divide_kernel,
        [(CHIPS, QUARTER, WIDTH)] + [(HALF, BLOCK, WIDTH)] * 2,
        [VMEM],
        (VMEM,) * 3,
        mib=8,
    )(both)


def tie(arrays, *after):
    count = len(arrays)
    return pl.pallas_call(
        lambda *refs: None,
        out_shape=tuple(jax.ShapeDtypeStruct(array.shape, array.dtype) for array in arrays),
        in_specs=[ANYWHERE] * (count + len(after)),
        out_specs=(ANYWHERE,) * count,
        input_output_aliases={number: number for number in range(count)},
        compiler_params=pltpu.CompilerParams(vmem_limit_bytes=2**20),
    )(*arrays, *after)


PARTS = [(0, None), (1, None), (3, None), (2, 0), (2, 1)]
MEMBERS = 16


def dense_kernel(index_ref, second_ref, own_ref, *refs):
    *piece_refs, dense_ref, piece_ref = refs
    core0, y0 = own_ref[2], own_ref[3]
    for number, ref in enumerate(piece_refs):
        piece_ref[number * CHIPS : (number + 1) * CHIPS] = ref[...]
    side_of = lax.broadcasted_iota(jnp.int32, (QUARTER, WIDTH), 1) // BLOCK
    dense_ref[...] = jnp.zeros_like(dense_ref)
    for chunk in range(0, CHIPS, MEMBERS):
        molecules = [second_ref[(chunk + member) * CORES + core0] for member in range(MEMBERS)]
        places = [(((molecule & 1) ^ core0) << 7) + (molecule >> 1) for molecule in molecules]
        for y_off in range(Y):
            tiles = [piece_ref[place + y_off * CHIPS] for place in places]
            swapped = [swap_halves(tile) for tile in tiles]
            for side in range(2):
                k = (((y0 + y_off) & (Y - 1)) << 1) + side
                placed = []
                for row, molecule in enumerate(molecules, chunk):
                    index = index_ref[k, molecule]
                    place = (
                        pl.ds(row * QUARTER, QUARTER),
                        pl.ds(pl.multiple_of((index >> 1) << 7, WIDTH), WIDTH),
                    )
                    parity = index & 1
                    value = jnp.where(parity == side, tiles[row - chunk], swapped[row - chunk])
                    placed.append((place, jnp.where(side_of == parity, value, dense_ref[place])))
                for place, value in placed:
                    dense_ref[place] = value


def dense_panel(pieces, own, occ_index, second_map):
    shape = (CHIPS * QUARTER, BASIS)
    return call(
        dense_kernel,
        [shape],
        [SMEM] * 3 + [VMEM] * len(pieces),
        (VMEM,),
        [pltpu.VMEM((len(pieces) * CHIPS, QUARTER, WIDTH), jnp.bfloat16)],
        mib=8,
    )(occ_index.T, second_map, own, *pieces)[0]


def occupied_kernel(own_ref, dense_ref, *refs):
    *row_refs, out_ref, rows_ref = refs
    x0, core0 = own_ref[1], own_ref[2]
    for core_off in range(CORES):
        for (off, part), ref in zip(PARTS, row_refs[core_off * len(PARTS) :]):
            block = ((core0 ^ core_off) << 2) + ((x0 + off) & (X - 1))
            place = pl.multiple_of((block << 6) + (part or 0) * (BLOCK // 2), 32)
            rows_ref[pl.ds(place, ref.shape[0]), :] = ref[...]
    product = lax.dot_general(
        dense_ref[...], rows_ref[...], NT, preferred_element_type=jnp.float32
    ).astype(jnp.bfloat16)
    for chip in range(CHIPS):
        out_ref[chip] = product[chip * QUARTER : (chip + 1) * QUARTER]


def occupied(dense, rows, own):
    lanes = CORES * X * BLOCK
    return call(
        occupied_kernel,
        [(CHIPS, QUARTER, lanes)],
        [SMEM] + [VMEM] * (1 + len(rows)),
        (VMEM,),
        [pltpu.VMEM((lanes, BASIS), jnp.bfloat16)],
    )(own, dense, *rows)[0]


def virtual_kernel(core_off, index_ref, first_ref, own_ref, *refs):
    panel_refs, refs = refs[: 2 * len(PARTS)], refs[2 * len(PARTS) :]
    if core_off:
        table_ref, before_ref, out_hbm, out_ref, left_ref, right_ref, out_sems = refs
    else:
        rows_ref, out_ref, table_ref, left_ref, right_ref = refs
    core0, y0 = own_ref[2], own_ref[3]
    half_table = CHIPS * CORES // 2
    for slot in range(MOLECULES):
        z, x, core = slot // (X * CORES), slot // CORES % X, slot % CORES
        place = z * X + core * 2 + x // 2
        molecule = first_ref[slot]
        left_ref[molecule] = place + half_table * (x % 2)
        right_ref[molecule] = place + half_table * (1 - x % 2)
    if not core_off:
        for z, tile_at in itertools.product(range(Z), range(X)):
            lanes = slice(tile_at * WIDTH, (tile_at + 1) * WIDTH)
            tile = jnp.concatenate([rows_ref[z * X + x, :, lanes] for x in range(X)], axis=0)
            table_ref[z * X + tile_at] = tile
            table_ref[half_table + z * X + tile_at] = swap_halves(tile)

    def panel(y_off, chip):
        refs, chip = panel_refs[chip // HALF * len(PARTS) :], chip % HALF
        if y_off == 2:
            return refs[3 + chip // (HALF // 2)][chip % (HALF // 2)]
        return refs[{0: 0, 1: 1, 3: 2}[y_off]][chip]

    first_half = lax.broadcasted_iota(jnp.int32, (BLOCK, WIDTH), 1) < BLOCK
    written = []
    for z in range(Z):
        for x in range(X):
            molecule = (z * X + x) * CORES + (core0 ^ core_off)
            left = []
            for y in range(Y):
                k = ((y0 + y) & (Y - 1)) << 1
                one = left_ref[index_ref[k, molecule]]
                two = right_ref[index_ref[k + 1, molecule]]
                left.append(jnp.where(first_half, table_ref[one], table_ref[two]))
            right = [panel(y, z * X + x) for y in range(Y)]
            found = lax.dot_general(
                jnp.concatenate(left, axis=1), jnp.concatenate(right, axis=1), NT,
                preferred_element_type=jnp.float32,
            ).astype(jnp.bfloat16)
            found = jnp.concatenate([found, found], axis=1)
            place = slice((z * X + x) * WIDTH, (z * X + x + 1) * WIDTH)
            if core_off:
                found = jnp.where(first_half == (core0 == 0), before_ref[:, place], found)
            out_ref[:, place] = found
        if core_off:
            place = (slice(None), pl.ds(z * X * WIDTH, X * WIDTH))
            written.append(
                pltpu.make_async_copy(out_ref.at[place], out_hbm.at[place], out_sems.at[z])
            )
            written[-1].start()
    for copy in written:
        copy.wait()


def virtual(core_off, panels, own, virt_index, first_map, *rest):
    shape, table = (BLOCK, BASIS), (MOLECULES, BLOCK, WIDTH)
    scratch = [pltpu.SMEM((MOLECULES,), jnp.int32)] * 2
    if core_off:
        scratch = [pltpu.VMEM(shape, jnp.bfloat16), *scratch, pltpu.SemaphoreType.DMA((Z,))]
    return call(
        functools.partial(virtual_kernel, core_off),
        [shape] if core_off else [shape, table],
        [SMEM] * 3 + [VMEM] * (len(panels) + len(rest)),
        (ANYWHERE,) if core_off else (VMEM, VMEM),
        scratch,
    )(virt_index.T, first_map, own, *panels, *rest)


def shift(array, axis, by):
    size = SIZES[axis]
    return lax.ppermute(array, axis, [((i + by) % size, i) for i in range(size)])


def ring(array, axis, *between):
    after, before = shift(array, axis, 1), shift(array, axis, -1)
    if between:
        after, before = tie([after, before], *between)
    middle = array.shape[0] // 2
    low, high = shift(before[:middle], axis, -1), shift(after[middle:], axis, 1)
    return [array, after, before, low, high]


def exchange(array):
    return lax.all_to_all(array, ("z", "x"), split_axis=0, concat_axis=0, tiled=True)


def per_device(
    b_tensor, pair_mask, first_map, second_map, occ_blocks, occ_index, virt_blocks, virt_index
):
    own = jnp.stack([lax.axis_index(axis) for axis in SIZES]).astype(jnp.int32)
    both = exchange(spread(own, occ_blocks, virt_blocks))
    occ_plane, *virt_planes = divide(both)
    pieces = [occ_plane] + [shift(occ_plane, "y", by) for by in range(1, Y)]
    rows = ring(mask_rows(pair_mask, b_tensor), "x", occ_plane)
    rows = rows + [shift(part, "core", 1) for part in rows]
    virt_planes = tie(virt_planes, *pieces[1:])
    pieces = pieces + [shift(piece, "core", 1) for piece in pieces]
    half = occupied(dense_panel(pieces, own, occ_index, second_map), rows, own)
    mine, later = (ring(plane, "y", half) for plane in virt_planes)
    turned = exchange(*tie([half], *mine[1:3]))
    mine = tie(mine + later, turned)
    other = [shift(panel, "core", 1) for panel in mine]
    known = (own, virt_index, first_map)
    columns, table = virtual(0, mine, *known, turned)
    return virtual(1, other, *known, table, columns)[0][None]


def solution(mesh):
    shaped = Mesh(mesh.devices.reshape(Z, X, CORES, Y), tuple(SIZES))
    wide = ("z", "x", "core")
    placed = (
        P("y", wide, None),
        P("y", wide, None),
        P(),
        P(),
        P(wide, "y", None, None),
        P(),
        P(wide, "y", None, None),
        P(),
    )
    return jax.shard_map(
        per_device, mesh=shaped, in_specs=placed, out_specs=P("y", wide, None), check_vma=False
    )
```

```python
import functools
import itertools

import jax
import jax.numpy as jnp
from jax import lax
from jax.experimental import pallas as pl
from jax.experimental.pallas import tpu as pltpu
from jax.sharding import Mesh, PartitionSpec as P

Z, X, CORES, Y = 8, 4, 2, 4
SIZES = {"z": Z, "x": X, "core": CORES, "y": Y}
CHIPS = Z * X
BLOCK, WIDTH, QUARTER = 64, 128, 16
MOLECULES = CHIPS * CORES
BASIS = MOLECULES * BLOCK
ANYWHERE = pl.BlockSpec(memory_space=pl.ANY)
SMEM = pl.BlockSpec(memory_space=pltpu.SMEM)
VMEM = pl.BlockSpec(memory_space=pltpu.VMEM)
NT = (((1,), (1,)), ((), ()))


def swap_halves(tile):
    return jnp.concatenate([tile[:, BLOCK:], tile[:, :BLOCK]], axis=1)


def call(kernel, outs, in_specs, out_specs, scratch=(), mib=16):
    return pl.pallas_call(
        kernel,
        out_shape=tuple(jax.ShapeDtypeStruct(shape, jnp.bfloat16) for shape in outs),
        in_specs=in_specs,
        out_specs=out_specs,
        scratch_shapes=list(scratch),
        compiler_params=pltpu.CompilerParams(vmem_limit_bytes=mib * 2**20),
        cost_estimate=pl.CostEstimate(flops=2**10, bytes_accessed=2**10, transcendentals=0),
    )


def mask_kernel(mask_ref, b_ref, masked_ref):
    first_half = lax.broadcasted_iota(jnp.int32, (BLOCK, WIDTH), 1) < BLOCK
    for pair in range(MOLECULES // 2):
        weight = jnp.where(first_half, mask_ref[0, 0, 2 * pair], mask_ref[0, 0, 2 * pair + 1])
        place = slice(pair * WIDTH, (pair + 1) * WIDTH)
        masked_ref[:, place] = b_ref[0, :, place] * weight.astype(jnp.float32).astype(jnp.bfloat16)


def mask_rows(pair_mask, b_tensor):
    return call(mask_kernel, [(BLOCK, BASIS)], [SMEM, VMEM], (VMEM,), mib=8)(pair_mask, b_tensor)[0]


def spread_kernel(own_ref, occ_ref, virt_ref, spread_ref):
    del own_ref
    occ = jnp.concatenate([occ_ref[0, 0], occ_ref[0, 1]], axis=1)
    rows = jnp.concatenate([virt_ref[0, 0], virt_ref[0, 1]], axis=0).astype(jnp.float32)
    virt = rows.T.astype(jnp.bfloat16)
    for z, x in itertools.product(range(Z), range(X)):
        quarter = slice(x * QUARTER, (x + 1) * QUARTER)
        spread_ref[z * X + x, :QUARTER] = occ[quarter]
        spread_ref[z * X + x, QUARTER:] = virt[quarter]


def spread(own, occ_blocks, virt_blocks):
    return call(
        spread_kernel, [(CHIPS, 2 * QUARTER, WIDTH)], [SMEM, VMEM, VMEM], (VMEM,), mib=8
    )(own, occ_blocks, virt_blocks)[0]


def divide_kernel(both_ref, occ_ref, virt_ref):
    for chip in range(CHIPS):
        occ_ref[chip] = both_ref[chip, :QUARTER]
        virt_ref[chip] = both_ref[chip, QUARTER:]


def divide(both):
    return call(
        divide_kernel,
        [(CHIPS, QUARTER, WIDTH)] * 2,
        [VMEM],
        (VMEM, VMEM),
        mib=8,
    )(both)


def assemble_kernel(own_ref, *refs):
    *quarter_refs, out_ref = refs
    for off, ref in enumerate(quarter_refs):
        rows = pl.ds(pl.multiple_of(((own_ref[1] + off) & (X - 1)) * QUARTER, QUARTER), QUARTER)
        for chip in range(CHIPS):
            out_ref[chip, rows, :] = ref[chip]


def assemble(own, quarters):
    return call(
        assemble_kernel, [(CHIPS, BLOCK, WIDTH)], [SMEM] + [VMEM] * X, (VMEM,), mib=8
    )(own, *quarters)[0]


def tie(arrays, *after):
    count = len(arrays)
    return pl.pallas_call(
        lambda *refs: None,
        out_shape=tuple(jax.ShapeDtypeStruct(array.shape, array.dtype) for array in arrays),
        in_specs=[ANYWHERE] * (count + len(after)),
        out_specs=(ANYWHERE,) * count,
        input_output_aliases={number: number for number in range(count)},
        compiler_params=pltpu.CompilerParams(vmem_limit_bytes=2**20),
    )(*arrays, *after)


PARTS = [(0, None), (1, None), (3, None), (2, 0), (2, 1)]
MEMBERS = 16


def dense_kernel(index_ref, second_ref, own_ref, *refs):
    *piece_refs, dense_ref, piece_ref = refs
    core0, y0 = own_ref[2], own_ref[3]
    for number, ref in enumerate(piece_refs):
        piece_ref[number * CHIPS : (number + 1) * CHIPS] = ref[...]
    side_of = lax.broadcasted_iota(jnp.int32, (QUARTER, WIDTH), 1) // BLOCK
    dense_ref[...] = jnp.zeros_like(dense_ref)
    for chunk in range(0, CHIPS, MEMBERS):
        molecules = [second_ref[(chunk + member) * CORES + core0] for member in range(MEMBERS)]
        places = [(((molecule & 1) ^ core0) << 7) + (molecule >> 1) for molecule in molecules]
        for y_off in range(Y):
            tiles = [piece_ref[place + y_off * CHIPS] for place in places]
            swapped = [swap_halves(tile) for tile in tiles]
            for side in range(2):
                k = (((y0 + y_off) & (Y - 1)) << 1) + side
                placed = []
                for row, molecule in enumerate(molecules, chunk):
                    index = index_ref[k, molecule]
                    place = (
                        pl.ds(row * QUARTER, QUARTER),
                        pl.ds(pl.multiple_of((index >> 1) << 7, WIDTH), WIDTH),
                    )
                    parity = index & 1
                    value = jnp.where(parity == side, tiles[row - chunk], swapped[row - chunk])
                    placed.append((place, jnp.where(side_of == parity, value, dense_ref[place])))
                for place, value in placed:
                    dense_ref[place] = value


def dense_panel(pieces, own, occ_index, second_map):
    shape = (CHIPS * QUARTER, BASIS)
    return call(
        dense_kernel,
        [shape],
        [SMEM] * 3 + [VMEM] * len(pieces),
        (VMEM,),
        [pltpu.VMEM((len(pieces) * CHIPS, QUARTER, WIDTH), jnp.bfloat16)],
        mib=8,
    )(occ_index.T, second_map, own, *pieces)[0]


def occupied_kernel(own_ref, dense_ref, *refs):
    *row_refs, out_ref, rows_ref = refs
    x0, core0 = own_ref[1], own_ref[2]
    for core_off in range(CORES):
        for (off, part), ref in zip(PARTS, row_refs[core_off * len(PARTS) :]):
            block = ((core0 ^ core_off) << 2) + ((x0 + off) & (X - 1))
            place = pl.multiple_of((block << 6) + (part or 0) * (BLOCK // 2), 32)
            rows_ref[pl.ds(place, ref.shape[0]), :] = ref[...]
    product = lax.dot_general(
        dense_ref[...], rows_ref[...], NT, preferred_element_type=jnp.float32
    ).astype(jnp.bfloat16)
    for chip in range(CHIPS):
        out_ref[chip] = product[chip * QUARTER : (chip + 1) * QUARTER]


def occupied(dense, rows, own):
    lanes = CORES * X * BLOCK
    return call(
        occupied_kernel,
        [(CHIPS, QUARTER, lanes)],
        [SMEM] + [VMEM] * (1 + len(rows)),
        (VMEM,),
        [pltpu.VMEM((lanes, BASIS), jnp.bfloat16)],
    )(own, dense, *rows)[0]


def virtual_kernel(core_off, index_ref, first_ref, own_ref, *refs):
    panel_refs, refs = refs[: len(PARTS)], refs[len(PARTS) :]
    if core_off:
        table_ref, before_ref, out_hbm, out_ref, left_ref, right_ref, out_sems = refs
    else:
        rows_ref, out_ref, table_ref, left_ref, right_ref = refs
    core0, y0 = own_ref[2], own_ref[3]
    half_table = CHIPS * CORES // 2
    for slot in range(MOLECULES):
        z, x, core = slot // (X * CORES), slot // CORES % X, slot % CORES
        place = z * X + core * 2 + x // 2
        molecule = first_ref[slot]
        left_ref[molecule] = place + half_table * (x % 2)
        right_ref[molecule] = place + half_table * (1 - x % 2)
    if not core_off:
        for z, tile_at in itertools.product(range(Z), range(X)):
            lanes = slice(tile_at * WIDTH, (tile_at + 1) * WIDTH)
            tile = jnp.concatenate([rows_ref[z * X + x, :, lanes] for x in range(X)], axis=0)
            table_ref[z * X + tile_at] = tile
            table_ref[half_table + z * X + tile_at] = swap_halves(tile)

    def panel(y_off, chip):
        if y_off == 2:
            return panel_refs[3 + chip // (CHIPS // 2)][chip % (CHIPS // 2)]
        return panel_refs[{0: 0, 1: 1, 3: 2}[y_off]][chip]

    first_half = lax.broadcasted_iota(jnp.int32, (BLOCK, WIDTH), 1) < BLOCK
    written = []
    for z in range(Z):
        for x in range(X):
            molecule = (z * X + x) * CORES + (core0 ^ core_off)
            left = []
            for y in range(Y):
                k = ((y0 + y) & (Y - 1)) << 1
                one = left_ref[index_ref[k, molecule]]
                two = right_ref[index_ref[k + 1, molecule]]
                left.append(jnp.where(first_half, table_ref[one], table_ref[two]))
            right = [panel(y, z * X + x) for y in range(Y)]
            found = lax.dot_general(
                jnp.concatenate(left, axis=1), jnp.concatenate(right, axis=1), NT,
                preferred_element_type=jnp.float32,
            ).astype(jnp.bfloat16)
            found = jnp.concatenate([found, found], axis=1)
            place = slice((z * X + x) * WIDTH, (z * X + x + 1) * WIDTH)
            if core_off:
                found = jnp.where(first_half == (core0 == 0), before_ref[:, place], found)
            out_ref[:, place] = found
        if core_off:
            place = (slice(None), pl.ds(z * X * WIDTH, X * WIDTH))
            written.append(
                pltpu.make_async_copy(out_ref.at[place], out_hbm.at[place], out_sems.at[z])
            )
            written[-1].start()
    for copy in written:
        copy.wait()


def virtual(core_off, panels, own, virt_index, first_map, *rest):
    shape, table = (BLOCK, BASIS), (MOLECULES, BLOCK, WIDTH)
    scratch = [pltpu.SMEM((MOLECULES,), jnp.int32)] * 2
    if core_off:
        scratch = [pltpu.VMEM(shape, jnp.bfloat16), *scratch, pltpu.SemaphoreType.DMA((Z,))]
    return call(
        functools.partial(virtual_kernel, core_off),
        [shape] if core_off else [shape, table],
        [SMEM] * 3 + [VMEM] * (len(panels) + len(rest)),
        (ANYWHERE,) if core_off else (VMEM, VMEM),
        scratch,
    )(virt_index.T, first_map, own, *panels, *rest)


def shift(array, axis, by):
    size = SIZES[axis]
    return lax.ppermute(array, axis, [((i + by) % size, i) for i in range(size)])


def ring(array, axis, *between):
    after, before = shift(array, axis, 1), shift(array, axis, -1)
    if between:
        after, before = tie([after, before], *between)
    middle = array.shape[0] // 2
    low, high = shift(before[:middle], axis, -1), shift(after[middle:], axis, 1)
    return [array, after, before, low, high]


def exchange(array):
    return lax.all_to_all(array, ("z", "x"), split_axis=0, concat_axis=0, tiled=True)


def per_device(
    b_tensor, pair_mask, first_map, second_map, occ_blocks, occ_index, virt_blocks, virt_index
):
    own = jnp.stack([lax.axis_index(axis) for axis in SIZES]).astype(jnp.int32)
    both = exchange(spread(own, occ_blocks, virt_blocks))
    occ_plane, virt_quarter = divide(both)
    pieces = [occ_plane] + [shift(occ_plane, "y", by) for by in range(1, Y)]
    rows = ring(mask_rows(pair_mask, b_tensor), "x", occ_plane)
    rows = rows + [shift(part, "core", 1) for part in rows]
    quarters = [virt_quarter] + [shift(virt_quarter, "x", by) for by in range(1, X)]
    virt_plane = assemble(own, quarters)
    pieces = pieces + [shift(piece, "core", 1) for piece in pieces]
    half = occupied(dense_panel(pieces, own, occ_index, second_map), rows, own)
    mine = ring(virt_plane, "y", half)
    turned = exchange(*tie([half], *mine[1:3]))
    mine = tie(mine, turned)
    other = [shift(panel, "core", 1) for panel in mine]
    known = (own, virt_index, first_map)
    columns, table = virtual(0, mine, *known, turned)
    return virtual(1, other, *known, table, columns)[0][None]


def solution(mesh):
    shaped = Mesh(mesh.devices.reshape(Z, X, CORES, Y), tuple(SIZES))
    wide = ("z", "x", "core")
    placed = (
        P("y", wide, None),
        P("y", wide, None),
        P(),
        P(),
        P(wide, "y", None, None),
        P(),
        P(wide, "y", None, None),
        P(),
    )
    return jax.shard_map(
        per_device, mesh=shaped, in_specs=placed, out_specs=P("y", wide, None), check_vma=False
    )
```

```python
import functools
import itertools

import jax
import jax.numpy as jnp
from jax import lax
from jax.experimental import pallas as pl
from jax.experimental.pallas import tpu as pltpu
from jax.sharding import Mesh, PartitionSpec as P

Z, X, CORES, Y = 8, 4, 2, 4
SIZES = {"z": Z, "x": X, "core": CORES, "y": Y}
CHIPS = Z * X
BLOCK, WIDTH, QUARTER = 64, 128, 16
MOLECULES = CHIPS * CORES
BASIS = MOLECULES * BLOCK
ANYWHERE = pl.BlockSpec(memory_space=pl.ANY)
SMEM = pl.BlockSpec(memory_space=pltpu.SMEM)
VMEM = pl.BlockSpec(memory_space=pltpu.VMEM)
NT = (((1,), (1,)), ((), ()))


def swap_halves(tile):
    return jnp.concatenate([tile[:, BLOCK:], tile[:, :BLOCK]], axis=1)


def call(kernel, outs, in_specs, out_specs, scratch=(), mib=16):
    return pl.pallas_call(
        kernel,
        out_shape=tuple(jax.ShapeDtypeStruct(shape, jnp.bfloat16) for shape in outs),
        in_specs=in_specs,
        out_specs=out_specs,
        scratch_shapes=list(scratch),
        compiler_params=pltpu.CompilerParams(vmem_limit_bytes=mib * 2**20),
        cost_estimate=pl.CostEstimate(flops=2**10, bytes_accessed=2**10, transcendentals=0),
    )


def mask_kernel(mask_ref, b_ref, masked_ref):
    first_half = lax.broadcasted_iota(jnp.int32, (BLOCK, WIDTH), 1) < BLOCK
    for pair in range(MOLECULES // 2):
        weight = jnp.where(first_half, mask_ref[0, 0, 2 * pair], mask_ref[0, 0, 2 * pair + 1])
        place = slice(pair * WIDTH, (pair + 1) * WIDTH)
        masked_ref[:, place] = b_ref[0, :, place] * weight.astype(jnp.float32).astype(jnp.bfloat16)


def mask_rows(pair_mask, b_tensor):
    return call(mask_kernel, [(BLOCK, BASIS)], [SMEM, VMEM], (VMEM,), mib=8)(pair_mask, b_tensor)[0]


def spread_kernel(own_ref, occ_ref, virt_ref, spread_ref):
    del own_ref
    occ = jnp.concatenate([occ_ref[0, 0], occ_ref[0, 1]], axis=1)
    rows = jnp.concatenate([virt_ref[0, 0], virt_ref[0, 1]], axis=0).astype(jnp.float32)
    virt = rows.T.astype(jnp.bfloat16)
    for z, x in itertools.product(range(Z), range(X)):
        quarter = slice(x * QUARTER, (x + 1) * QUARTER)
        spread_ref[z * X + x, :QUARTER] = occ[quarter]
        spread_ref[z * X + x, QUARTER:] = virt[quarter]


def spread(own, occ_blocks, virt_blocks):
    return call(
        spread_kernel, [(CHIPS, 2 * QUARTER, WIDTH)], [SMEM, VMEM, VMEM], (VMEM,), mib=8
    )(own, occ_blocks, virt_blocks)[0]


def divide_kernel(both_ref, occ_ref, virt_ref):
    for chip in range(CHIPS):
        occ_ref[chip] = both_ref[chip, :QUARTER]
        virt_ref[chip] = both_ref[chip, QUARTER:]


def divide(both):
    return call(
        divide_kernel,
        [(CHIPS, QUARTER, WIDTH)] * 2,
        [VMEM],
        (VMEM, VMEM),
        mib=8,
    )(both)


def assemble_kernel(own_ref, *refs):
    *quarter_refs, out_ref = refs
    for off, ref in enumerate(quarter_refs):
        rows = pl.ds(pl.multiple_of(((own_ref[1] + off) & (X - 1)) * QUARTER, QUARTER), QUARTER)
        for chip in range(CHIPS):
            out_ref[chip, rows, :] = ref[chip]


def assemble(own, quarters):
    return call(
        assemble_kernel, [(CHIPS, BLOCK, WIDTH)], [SMEM] + [VMEM] * X, (VMEM,), mib=8
    )(own, *quarters)[0]


def tie(arrays, *after):
    count = len(arrays)
    return pl.pallas_call(
        lambda *refs: None,
        out_shape=tuple(jax.ShapeDtypeStruct(array.shape, array.dtype) for array in arrays),
        in_specs=[ANYWHERE] * (count + len(after)),
        out_specs=(ANYWHERE,) * count,
        input_output_aliases={number: number for number in range(count)},
        compiler_params=pltpu.CompilerParams(vmem_limit_bytes=2**20),
    )(*arrays, *after)


PARTS = [(0, None), (1, None), (3, None), (2, 0), (2, 1)]
MEMBERS = 16


def dense_kernel(index_ref, second_ref, own_ref, *refs):
    *piece_refs, dense_ref, piece_ref = refs
    core0, y0 = own_ref[2], own_ref[3]
    for number, ref in enumerate(piece_refs):
        piece_ref[number * CHIPS : (number + 1) * CHIPS] = ref[...]
    side_of = lax.broadcasted_iota(jnp.int32, (QUARTER, WIDTH), 1) // BLOCK
    dense_ref[...] = jnp.zeros_like(dense_ref)
    for chunk in range(0, CHIPS, MEMBERS):
        molecules = [second_ref[(chunk + member) * CORES + core0] for member in range(MEMBERS)]
        places = [(((molecule & 1) ^ core0) << 7) + (molecule >> 1) for molecule in molecules]
        for y_off in range(Y):
            tiles = [piece_ref[place + y_off * CHIPS] for place in places]
            swapped = [swap_halves(tile) for tile in tiles]
            for side in range(2):
                k = (((y0 + y_off) & (Y - 1)) << 1) + side
                placed = []
                for row, molecule in enumerate(molecules, chunk):
                    index = index_ref[k, molecule]
                    place = (
                        pl.ds(row * QUARTER, QUARTER),
                        pl.ds(pl.multiple_of((index >> 1) << 7, WIDTH), WIDTH),
                    )
                    parity = index & 1
                    value = jnp.where(parity == side, tiles[row - chunk], swapped[row - chunk])
                    placed.append((place, jnp.where(side_of == parity, value, dense_ref[place])))
                for place, value in placed:
                    dense_ref[place] = value


def dense_panel(pieces, own, occ_index, second_map):
    shape = (CHIPS * QUARTER, BASIS)
    return call(
        dense_kernel,
        [shape],
        [SMEM] * 3 + [VMEM] * len(pieces),
        (VMEM,),
        [pltpu.VMEM((len(pieces) * CHIPS, QUARTER, WIDTH), jnp.bfloat16)],
        mib=8,
    )(occ_index.T, second_map, own, *pieces)[0]


def occupied_kernel(own_ref, dense_ref, *refs):
    *row_refs, out_ref, rows_ref = refs
    x0, core0 = own_ref[1], own_ref[2]
    for core_off in range(CORES):
        for (off, part), ref in zip(PARTS, row_refs[core_off * len(PARTS) :]):
            block = ((core0 ^ core_off) << 2) + ((x0 + off) & (X - 1))
            place = pl.multiple_of((block << 6) + (part or 0) * (BLOCK // 2), 32)
            rows_ref[pl.ds(place, ref.shape[0]), :] = ref[...]
    product = lax.dot_general(
        dense_ref[...], rows_ref[...], NT, preferred_element_type=jnp.float32
    ).astype(jnp.bfloat16)
    for chip in range(CHIPS):
        out_ref[chip] = product[chip * QUARTER : (chip + 1) * QUARTER]


def occupied(dense, rows, own):
    lanes = CORES * X * BLOCK
    return call(
        occupied_kernel,
        [(CHIPS, QUARTER, lanes)],
        [SMEM] + [VMEM] * (1 + len(rows)),
        (VMEM,),
        [pltpu.VMEM((lanes, BASIS), jnp.bfloat16)],
    )(own, dense, *rows)[0]


def virtual_kernel(core_off, index_ref, first_ref, own_ref, *refs):
    panel_refs, refs = refs[: len(PARTS)], refs[len(PARTS) :]
    if core_off:
        table_ref, before_ref, out_hbm, out_ref, left_ref, right_ref, out_sems = refs
    else:
        rows_ref, out_ref, table_ref, left_ref, right_ref = refs
    core0, y0 = own_ref[2], own_ref[3]
    half_table = CHIPS * CORES // 2
    for slot in range(MOLECULES):
        z, x, core = slot // (X * CORES), slot // CORES % X, slot % CORES
        place = z * X + core * 2 + x // 2
        molecule = first_ref[slot]
        left_ref[molecule] = place + half_table * (x % 2)
        right_ref[molecule] = place + half_table * (1 - x % 2)
    if not core_off:
        for z, tile_at in itertools.product(range(Z), range(X)):
            lanes = slice(tile_at * WIDTH, (tile_at + 1) * WIDTH)
            tile = jnp.concatenate([rows_ref[z * X + x, :, lanes] for x in range(X)], axis=0)
            table_ref[z * X + tile_at] = tile
            table_ref[half_table + z * X + tile_at] = swap_halves(tile)

    def panel(y_off, chip):
        if y_off == 2:
            return panel_refs[3 + chip // (CHIPS // 2)][chip % (CHIPS // 2)]
        return panel_refs[{0: 0, 1: 1, 3: 2}[y_off]][chip]

    first_half = lax.broadcasted_iota(jnp.int32, (BLOCK, WIDTH), 1) < BLOCK
    written = []
    for z in range(Z):
        for x in range(X):
            molecule = (z * X + x) * CORES + (core0 ^ core_off)
            left = []
            for y in range(Y):
                k = ((y0 + y) & (Y - 1)) << 1
                one = left_ref[index_ref[k, molecule]]
                two = right_ref[index_ref[k + 1, molecule]]
                left.append(jnp.where(first_half, table_ref[one], table_ref[two]))
            right = [panel(y, z * X + x) for y in range(Y)]
            found = lax.dot_general(
                jnp.concatenate(left, axis=1), jnp.concatenate(right, axis=1), NT,
                preferred_element_type=jnp.float32,
            ).astype(jnp.bfloat16)
            found = jnp.concatenate([found, found], axis=1)
            place = slice((z * X + x) * WIDTH, (z * X + x + 1) * WIDTH)
            if core_off:
                found = jnp.where(first_half == (core0 == 0), before_ref[:, place], found)
            out_ref[:, place] = found
        if core_off:
            place = (slice(None), pl.ds(z * X * WIDTH, X * WIDTH))
            written.append(
                pltpu.make_async_copy(out_ref.at[place], out_hbm.at[place], out_sems.at[z])
            )
            written[-1].start()
    for copy in written:
        copy.wait()


def virtual(core_off, panels, own, virt_index, first_map, *rest):
    shape, table = (BLOCK, BASIS), (MOLECULES, BLOCK, WIDTH)
    scratch = [pltpu.SMEM((MOLECULES,), jnp.int32)] * 2
    if core_off:
        scratch = [pltpu.VMEM(shape, jnp.bfloat16), *scratch, pltpu.SemaphoreType.DMA((Z,))]
    return call(
        functools.partial(virtual_kernel, core_off),
        [shape] if core_off else [shape, table],
        [SMEM] * 3 + [VMEM] * (len(panels) + len(rest)),
        (ANYWHERE,) if core_off else (VMEM, VMEM),
        scratch,
    )(virt_index.T, first_map, own, *panels, *rest)


def shift(array, axis, by):
    size = SIZES[axis]
    return lax.ppermute(array, axis, [((i + by) % size, i) for i in range(size)])


def ring(array, axis, *between):
    after, before = shift(array, axis, 1), shift(array, axis, -1)
    if between:
        after, before = tie([after, before], *between)
    middle = array.shape[0] // 2
    low, high = shift(before[:middle], axis, -1), shift(after[middle:], axis, 1)
    return [array, after, before, low, high]


def exchange(array):
    return lax.all_to_all(array, ("z", "x"), split_axis=0, concat_axis=0, tiled=True)


def per_device(
    b_tensor, pair_mask, first_map, second_map, occ_blocks, occ_index, virt_blocks, virt_index
):
    own = jnp.stack([lax.axis_index(axis) for axis in SIZES]).astype(jnp.int32)
    both = exchange(spread(own, occ_blocks, virt_blocks))
    occ_plane, virt_quarter = divide(both)
    pieces = [occ_plane] + [shift(occ_plane, "y", by) for by in range(1, Y)]
    rows = ring(mask_rows(pair_mask, b_tensor), "x", occ_plane)
    rows = rows + [shift(part, "core", 1) for part in rows]
    (virt_quarter,) = tie([virt_quarter], *rows[3:5])
    quarters = [virt_quarter] + [shift(virt_quarter, "x", by) for by in range(1, X)]
    virt_plane = assemble(own, quarters)
    pieces = pieces + [shift(piece, "core", 1) for piece in pieces]
    half = occupied(dense_panel(pieces, own, occ_index, second_map), rows, own)
    mine = ring(virt_plane, "y", half)
    turned = exchange(*tie([half], virt_plane))
    mine = tie(mine, turned)
    other = [shift(panel, "core", 1) for panel in mine]
    known = (own, virt_index, first_map)
    columns, table = virtual(0, mine, *known, turned)
    return virtual(1, other, *known, table, columns)[0][None]


def solution(mesh):
    shaped = Mesh(mesh.devices.reshape(Z, X, CORES, Y), tuple(SIZES))
    wide = ("z", "x", "core")
    placed = (
        P("y", wide, None),
        P("y", wide, None),
        P(),
        P(),
        P(wide, "y", None, None),
        P(),
        P(wide, "y", None, None),
        P(),
    )
    return jax.shard_map(
        per_device, mesh=shaped, in_specs=placed, out_specs=P("y", wide, None), check_vma=False
    )
```

```python
import functools
import itertools

import jax
import jax.numpy as jnp
from jax import lax
from jax.experimental import pallas as pl
from jax.experimental.pallas import tpu as pltpu
from jax.sharding import Mesh, PartitionSpec as P

Z, X, CORES, Y = 8, 4, 2, 4
SIZES = {"z": Z, "x": X, "core": CORES, "y": Y}
CHIPS = Z * X
BLOCK, WIDTH, QUARTER = 64, 128, 16
MOLECULES = CHIPS * CORES
BASIS = MOLECULES * BLOCK
ANYWHERE = pl.BlockSpec(memory_space=pl.ANY)
SMEM = pl.BlockSpec(memory_space=pltpu.SMEM)
VMEM = pl.BlockSpec(memory_space=pltpu.VMEM)
NT = (((1,), (1,)), ((), ()))


def swap_halves(tile):
    return jnp.concatenate([tile[:, BLOCK:], tile[:, :BLOCK]], axis=1)


def call(kernel, outs, in_specs, out_specs, scratch=(), mib=16):
    return pl.pallas_call(
        kernel,
        out_shape=tuple(jax.ShapeDtypeStruct(shape, jnp.bfloat16) for shape in outs),
        in_specs=in_specs,
        out_specs=out_specs,
        scratch_shapes=list(scratch),
        compiler_params=pltpu.CompilerParams(vmem_limit_bytes=mib * 2**20),
        cost_estimate=pl.CostEstimate(flops=2**10, bytes_accessed=2**10, transcendentals=0),
    )


def mask_kernel(mask_ref, b_ref, masked_ref):
    first_half = lax.broadcasted_iota(jnp.int32, (BLOCK, WIDTH), 1) < BLOCK
    for pair in range(MOLECULES // 2):
        weight = jnp.where(first_half, mask_ref[0, 0, 2 * pair], mask_ref[0, 0, 2 * pair + 1])
        place = slice(pair * WIDTH, (pair + 1) * WIDTH)
        masked_ref[:, place] = b_ref[0, :, place] * weight.astype(jnp.float32).astype(jnp.bfloat16)


def mask_rows(pair_mask, b_tensor):
    return call(mask_kernel, [(BLOCK, BASIS)], [SMEM, VMEM], (VMEM,), mib=8)(pair_mask, b_tensor)[0]


def spread_kernel(own_ref, occ_ref, virt_ref, spread_ref):
    del own_ref
    occ = jnp.concatenate([occ_ref[0, 0], occ_ref[0, 1]], axis=1)
    rows = jnp.concatenate([virt_ref[0, 0], virt_ref[0, 1]], axis=0).astype(jnp.float32)
    virt = rows.T.astype(jnp.bfloat16)
    for z, x in itertools.product(range(Z), range(X)):
        spread_ref[z * X + x, :QUARTER] = occ[x * QUARTER : (x + 1) * QUARTER]
        spread_ref[z * X + x, QUARTER:] = virt


def spread(own, occ_blocks, virt_blocks):
    return call(
        spread_kernel, [(CHIPS, QUARTER + BLOCK, WIDTH)], [SMEM, VMEM, VMEM], (VMEM,), mib=8
    )(own, occ_blocks, virt_blocks)[0]


def divide_kernel(both_ref, occ_ref, virt_ref):
    for chip in range(CHIPS):
        occ_ref[chip] = both_ref[chip, :QUARTER]
        virt_ref[chip] = both_ref[chip, QUARTER:]


def divide(both):
    return call(
        divide_kernel,
        [(CHIPS, QUARTER, WIDTH), (CHIPS, BLOCK, WIDTH)],
        [VMEM],
        (VMEM, VMEM),
        mib=8,
    )(both)


def tie(arrays, *after):
    count = len(arrays)
    return pl.pallas_call(
        lambda *refs: None,
        out_shape=tuple(jax.ShapeDtypeStruct(array.shape, array.dtype) for array in arrays),
        in_specs=[ANYWHERE] * (count + len(after)),
        out_specs=(ANYWHERE,) * count,
        input_output_aliases={number: number for number in range(count)},
        compiler_params=pltpu.CompilerParams(vmem_limit_bytes=2**20),
    )(*arrays, *after)


PARTS = [(0, None), (1, None), (3, None), (2, 0), (2, 1)]
MEMBERS = 16


def dense_kernel(index_ref, second_ref, own_ref, *refs):
    *piece_refs, dense_ref, piece_ref = refs
    core0, y0 = own_ref[2], own_ref[3]
    for number, ref in enumerate(piece_refs):
        piece_ref[number * CHIPS : (number + 1) * CHIPS] = ref[...]
    side_of = lax.broadcasted_iota(jnp.int32, (QUARTER, WIDTH), 1) // BLOCK
    dense_ref[...] = jnp.zeros_like(dense_ref)
    for chunk in range(0, CHIPS, MEMBERS):
        molecules = [second_ref[(chunk + member) * CORES + core0] for member in range(MEMBERS)]
        places = [(((molecule & 1) ^ core0) << 7) + (molecule >> 1) for molecule in molecules]
        for y_off in range(Y):
            tiles = [piece_ref[place + y_off * CHIPS] for place in places]
            swapped = [swap_halves(tile) for tile in tiles]
            for side in range(2):
                k = (((y0 + y_off) & (Y - 1)) << 1) + side
                placed = []
                for row, molecule in enumerate(molecules, chunk):
                    index = index_ref[k, molecule]
                    place = (
                        pl.ds(row * QUARTER, QUARTER),
                        pl.ds(pl.multiple_of((index >> 1) << 7, WIDTH), WIDTH),
                    )
                    parity = index & 1
                    value = jnp.where(parity == side, tiles[row - chunk], swapped[row - chunk])
                    placed.append((place, jnp.where(side_of == parity, value, dense_ref[place])))
                for place, value in placed:
                    dense_ref[place] = value


def dense_panel(pieces, own, occ_index, second_map):
    shape = (CHIPS * QUARTER, BASIS)
    return call(
        dense_kernel,
        [shape],
        [SMEM] * 3 + [VMEM] * len(pieces),
        (VMEM,),
        [pltpu.VMEM((len(pieces) * CHIPS, QUARTER, WIDTH), jnp.bfloat16)],
        mib=8,
    )(occ_index.T, second_map, own, *pieces)[0]


def occupied_kernel(own_ref, dense_ref, *refs):
    row_refs, (out_ref, rows_ref) = refs[: CORES * len(PARTS)], refs[-2:]
    x0, core0 = own_ref[1], own_ref[2]
    for core_off in range(CORES):
        for (off, part), ref in zip(PARTS, row_refs[core_off * len(PARTS) :]):
            block = ((core0 ^ core_off) << 2) + ((x0 + off) & (X - 1))
            place = pl.multiple_of((block << 6) + (part or 0) * (BLOCK // 2), 32)
            rows_ref[pl.ds(place, ref.shape[0]), :] = ref[...]
    product = lax.dot_general(
        dense_ref[...], rows_ref[...], NT, preferred_element_type=jnp.float32
    ).astype(jnp.bfloat16)
    for chip in range(CHIPS):
        out_ref[chip] = product[chip * QUARTER : (chip + 1) * QUARTER]


def occupied(dense, rows, own, *early):
    lanes = CORES * X * BLOCK
    return call(
        occupied_kernel,
        [(CHIPS, QUARTER, lanes)],
        [SMEM] + [VMEM] * (1 + len(rows)) + [ANYWHERE] * len(early),
        (VMEM,),
        [pltpu.VMEM((lanes, BASIS), jnp.bfloat16)],
    )(own, dense, *rows, *early)[0]


def virtual_kernel(core_off, index_ref, first_ref, own_ref, *refs):
    panel_refs, refs = refs[: len(PARTS)], refs[len(PARTS) :]
    if core_off:
        table_ref, before_ref, out_hbm, out_ref, left_ref, right_ref, out_sems = refs
    else:
        rows_ref, out_ref, table_ref, left_ref, right_ref = refs
    core0, y0 = own_ref[2], own_ref[3]
    half_table = CHIPS * CORES // 2
    for slot in range(MOLECULES):
        z, x, core = slot // (X * CORES), slot // CORES % X, slot % CORES
        place = z * X + core * 2 + x // 2
        molecule = first_ref[slot]
        left_ref[molecule] = place + half_table * (x % 2)
        right_ref[molecule] = place + half_table * (1 - x % 2)
    if not core_off:
        for z, tile_at in itertools.product(range(Z), range(X)):
            lanes = slice(tile_at * WIDTH, (tile_at + 1) * WIDTH)
            tile = jnp.concatenate([rows_ref[z * X + x, :, lanes] for x in range(X)], axis=0)
            table_ref[z * X + tile_at] = tile
            table_ref[half_table + z * X + tile_at] = swap_halves(tile)

    def panel(y_off, chip):
        if y_off == 2:
            return panel_refs[3 + chip // (CHIPS // 2)][chip % (CHIPS // 2)]
        return panel_refs[{0: 0, 1: 1, 3: 2}[y_off]][chip]

    first_half = lax.broadcasted_iota(jnp.int32, (BLOCK, WIDTH), 1) < BLOCK
    written = []
    for z in range(Z):
        for x in range(X):
            molecule = (z * X + x) * CORES + (core0 ^ core_off)
            left = []
            for y in range(Y):
                k = ((y0 + y) & (Y - 1)) << 1
                one = left_ref[index_ref[k, molecule]]
                two = right_ref[index_ref[k + 1, molecule]]
                left.append(jnp.where(first_half, table_ref[one], table_ref[two]))
            right = [panel(y, z * X + x) for y in range(Y)]
            found = lax.dot_general(
                jnp.concatenate(left, axis=1), jnp.concatenate(right, axis=1), NT,
                preferred_element_type=jnp.float32,
            ).astype(jnp.bfloat16)
            found = jnp.concatenate([found, found], axis=1)
            place = slice((z * X + x) * WIDTH, (z * X + x + 1) * WIDTH)
            if core_off:
                found = jnp.where(first_half == (core0 == 0), before_ref[:, place], found)
            out_ref[:, place] = found
        if core_off:
            place = (slice(None), pl.ds(z * X * WIDTH, X * WIDTH))
            written.append(
                pltpu.make_async_copy(out_ref.at[place], out_hbm.at[place], out_sems.at[z])
            )
            written[-1].start()
    for copy in written:
        copy.wait()


def virtual(core_off, panels, own, virt_index, first_map, *rest):
    shape, table = (BLOCK, BASIS), (MOLECULES, BLOCK, WIDTH)
    scratch = [pltpu.SMEM((MOLECULES,), jnp.int32)] * 2
    if core_off:
        scratch = [pltpu.VMEM(shape, jnp.bfloat16), *scratch, pltpu.SemaphoreType.DMA((Z,))]
    return call(
        functools.partial(virtual_kernel, core_off),
        [shape] if core_off else [shape, table],
        [SMEM] * 3 + [VMEM] * (len(panels) + len(rest)),
        (ANYWHERE,) if core_off else (VMEM, VMEM),
        scratch,
    )(virt_index.T, first_map, own, *panels, *rest)


def shift(array, axis, by):
    size = SIZES[axis]
    return lax.ppermute(array, axis, [((i + by) % size, i) for i in range(size)])


def second_step(neighbours, axis):
    after, before = neighbours
    middle = after.shape[0] // 2
    low, high = shift(before[:middle], axis, -1), shift(after[middle:], axis, 1)
    return [after, before, low, high]


def exchange(array):
    return lax.all_to_all(array, ("z", "x"), split_axis=0, concat_axis=0, tiled=True)


def per_device(
    b_tensor, pair_mask, first_map, second_map, occ_blocks, occ_index, virt_blocks, virt_index
):
    own = jnp.stack([lax.axis_index(axis) for axis in SIZES]).astype(jnp.int32)
    both = exchange(spread(own, occ_blocks, virt_blocks))
    occ_plane, virt_plane = divide(both)
    pieces = [occ_plane] + [shift(occ_plane, "y", by) for by in range(1, Y)]
    masked = mask_rows(pair_mask, b_tensor)
    ahead = [shift(masked, "x", 1), shift(masked, "x", -1)]
    rows = [masked, *second_step(tie(ahead, occ_plane), "x")]
    rows = rows + [shift(part, "core", 1) for part in rows]
    (virt_plane,) = tie([virt_plane], *rows[1:3])
    ahead = [shift(virt_plane, "y", 1), shift(virt_plane, "y", -1)]
    pieces = pieces + [shift(piece, "core", 1) for piece in pieces]
    half = occupied(dense_panel(pieces, own, occ_index, second_map), rows, own, *ahead)
    turned = exchange(half)
    mine = [virt_plane, *second_step(tie(ahead, half), "y")]
    mine = tie(mine, turned)
    other = [shift(panel, "core", 1) for panel in mine]
    known = (own, virt_index, first_map)
    columns, table = virtual(0, mine, *known, turned)
    return virtual(1, other, *known, table, columns)[0][None]


def solution(mesh):
    shaped = Mesh(mesh.devices.reshape(Z, X, CORES, Y), tuple(SIZES))
    wide = ("z", "x", "core")
    placed = (
        P("y", wide, None),
        P("y", wide, None),
        P(),
        P(),
        P(wide, "y", None, None),
        P(),
        P(wide, "y", None, None),
        P(),
    )
    return jax.shard_map(
        per_device, mesh=shaped, in_specs=placed, out_specs=P("y", wide, None), check_vma=False
    )
```

```python
import functools
import itertools

import jax
import jax.numpy as jnp
from jax import lax
from jax.experimental import pallas as pl
from jax.experimental.pallas import tpu as pltpu
from jax.sharding import Mesh, PartitionSpec as P

Z, X, CORES, Y = 8, 4, 2, 4
SIZES = {"z": Z, "x": X, "core": CORES, "y": Y}
CHIPS = Z * X
BLOCK, WIDTH, QUARTER = 64, 128, 16
MOLECULES = CHIPS * CORES
BASIS = MOLECULES * BLOCK
ANYWHERE = pl.BlockSpec(memory_space=pl.ANY)
SMEM = pl.BlockSpec(memory_space=pltpu.SMEM)
VMEM = pl.BlockSpec(memory_space=pltpu.VMEM)
NT = (((1,), (1,)), ((), ()))


def swap_halves(tile):
    return jnp.concatenate([tile[:, BLOCK:], tile[:, :BLOCK]], axis=1)


def call(kernel, outs, in_specs, out_specs, scratch=(), mib=16):
    return pl.pallas_call(
        kernel,
        out_shape=tuple(jax.ShapeDtypeStruct(shape, jnp.bfloat16) for shape in outs),
        in_specs=in_specs,
        out_specs=out_specs,
        scratch_shapes=list(scratch),
        compiler_params=pltpu.CompilerParams(vmem_limit_bytes=mib * 2**20),
        cost_estimate=pl.CostEstimate(flops=2**10, bytes_accessed=2**10, transcendentals=0),
    )


def mask_kernel(mask_ref, b_ref, masked_ref):
    first_half = lax.broadcasted_iota(jnp.int32, (BLOCK, WIDTH), 1) < BLOCK
    for pair in range(MOLECULES // 2):
        weight = jnp.where(first_half, mask_ref[0, 0, 2 * pair], mask_ref[0, 0, 2 * pair + 1])
        place = slice(pair * WIDTH, (pair + 1) * WIDTH)
        masked_ref[:, place] = b_ref[0, :, place] * weight.astype(jnp.float32).astype(jnp.bfloat16)


def mask_rows(pair_mask, b_tensor):
    return call(mask_kernel, [(BLOCK, BASIS)], [SMEM, VMEM], (VMEM,), mib=8)(pair_mask, b_tensor)[0]


def spread_kernel(own_ref, occ_ref, virt_ref, spread_ref):
    del own_ref
    occ = jnp.concatenate([occ_ref[0, 0], occ_ref[0, 1]], axis=1)
    rows = jnp.concatenate([virt_ref[0, 0], virt_ref[0, 1]], axis=0).astype(jnp.float32)
    virt = rows.T.astype(jnp.bfloat16)
    for z, x in itertools.product(range(Z), range(X)):
        quarter = slice(x * QUARTER, (x + 1) * QUARTER)
        spread_ref[z * X + x, :QUARTER] = occ[quarter]
        spread_ref[z * X + x, QUARTER:] = virt[quarter]


def spread(own, occ_blocks, virt_blocks):
    return call(
        spread_kernel, [(CHIPS, 2 * QUARTER, WIDTH)], [SMEM, VMEM, VMEM], (VMEM,), mib=8
    )(own, occ_blocks, virt_blocks)[0]


def divide_kernel(both_ref, occ_ref, virt_ref):
    for chip in range(CHIPS):
        occ_ref[chip] = both_ref[chip, :QUARTER]
        virt_ref[chip] = both_ref[chip, QUARTER:]


def divide(both):
    return call(
        divide_kernel,
        [(CHIPS, QUARTER, WIDTH)] * 2,
        [VMEM],
        (VMEM, VMEM),
        mib=8,
    )(both)


def stack_kernel(*refs):
    *parts, out_ref = refs
    for y, ref in enumerate(parts):
        out_ref[y] = ref[...]


def stack(parts):
    return call(
        stack_kernel, [(Y, CHIPS, QUARTER, WIDTH)], [VMEM] * Y, (VMEM,), mib=8
    )(*parts)[0]


def tie(arrays, *after):
    count = len(arrays)
    return pl.pallas_call(
        lambda *refs: None,
        out_shape=tuple(jax.ShapeDtypeStruct(array.shape, array.dtype) for array in arrays),
        in_specs=[ANYWHERE] * (count + len(after)),
        out_specs=(ANYWHERE,) * count,
        input_output_aliases={number: number for number in range(count)},
        compiler_params=pltpu.CompilerParams(vmem_limit_bytes=2**20),
    )(*arrays, *after)


PARTS = [(0, None), (1, None), (3, None), (2, 0), (2, 1)]
MEMBERS = 16


def dense_kernel(index_ref, second_ref, own_ref, *refs):
    *piece_refs, dense_ref, piece_ref = refs
    core0, y0 = own_ref[2], own_ref[3]
    for number, ref in enumerate(piece_refs):
        piece_ref[number * CHIPS : (number + 1) * CHIPS] = ref[...]
    side_of = lax.broadcasted_iota(jnp.int32, (QUARTER, WIDTH), 1) // BLOCK
    dense_ref[...] = jnp.zeros_like(dense_ref)
    for chunk in range(0, CHIPS, MEMBERS):
        molecules = [second_ref[(chunk + member) * CORES + core0] for member in range(MEMBERS)]
        places = [(((molecule & 1) ^ core0) << 7) + (molecule >> 1) for molecule in molecules]
        for y_off in range(Y):
            tiles = [piece_ref[place + y_off * CHIPS] for place in places]
            swapped = [swap_halves(tile) for tile in tiles]
            for side in range(2):
                k = (((y0 + y_off) & (Y - 1)) << 1) + side
                placed = []
                for row, molecule in enumerate(molecules, chunk):
                    index = index_ref[k, molecule]
                    place = (
                        pl.ds(row * QUARTER, QUARTER),
                        pl.ds(pl.multiple_of((index >> 1) << 7, WIDTH), WIDTH),
                    )
                    parity = index & 1
                    value = jnp.where(parity == side, tiles[row - chunk], swapped[row - chunk])
                    placed.append((place, jnp.where(side_of == parity, value, dense_ref[place])))
                for place, value in placed:
                    dense_ref[place] = value


def dense_panel(pieces, own, occ_index, second_map):
    shape = (CHIPS * QUARTER, BASIS)
    return call(
        dense_kernel,
        [shape],
        [SMEM] * 3 + [VMEM] * len(pieces),
        (VMEM,),
        [pltpu.VMEM((len(pieces) * CHIPS, QUARTER, WIDTH), jnp.bfloat16)],
        mib=8,
    )(occ_index.T, second_map, own, *pieces)[0]


def occupied_kernel(own_ref, dense_ref, *refs):
    *row_refs, out_ref, rows_ref = refs
    x0, core0 = own_ref[1], own_ref[2]
    for core_off in range(CORES):
        for (off, part), ref in zip(PARTS, row_refs[core_off * len(PARTS) :]):
            block = ((core0 ^ core_off) << 2) + ((x0 + off) & (X - 1))
            place = pl.multiple_of((block << 6) + (part or 0) * (BLOCK // 2), 32)
            rows_ref[pl.ds(place, ref.shape[0]), :] = ref[...]
    product = lax.dot_general(
        dense_ref[...], rows_ref[...], NT, preferred_element_type=jnp.float32
    ).astype(jnp.bfloat16)
    for chip in range(CHIPS):
        out_ref[chip] = product[chip * QUARTER : (chip + 1) * QUARTER]


def occupied(dense, rows, own):
    lanes = CORES * X * BLOCK
    return call(
        occupied_kernel,
        [(CHIPS, QUARTER, lanes)],
        [SMEM] + [VMEM] * (1 + len(rows)),
        (VMEM,),
        [pltpu.VMEM((lanes, BASIS), jnp.bfloat16)],
    )(own, dense, *rows)[0]


def virtual_kernel(core_off, index_ref, first_ref, own_ref, *refs):
    panel_refs, refs = refs[: len(PARTS)], refs[len(PARTS) :]
    if core_off:
        table_ref, before_ref, out_hbm, out_ref, panel_ref, left_ref, right_ref, out_sems = refs
    else:
        rows_ref, out_ref, table_ref, panel_ref, left_ref, right_ref = refs
    x0, core0, y0 = (own_ref[i] for i in range(1, 4))
    half_table = CHIPS * CORES // 2
    for slot in range(MOLECULES):
        z, x, core = slot // (X * CORES), slot // CORES % X, slot % CORES
        place = z * X + core * 2 + x // 2
        molecule = first_ref[slot]
        left_ref[molecule] = place + half_table * (x % 2)
        right_ref[molecule] = place + half_table * (1 - x % 2)
    if not core_off:
        for z, tile_at in itertools.product(range(Z), range(X)):
            lanes = slice(tile_at * WIDTH, (tile_at + 1) * WIDTH)
            tile = jnp.concatenate([rows_ref[z * X + x, :, lanes] for x in range(X)], axis=0)
            table_ref[z * X + tile_at] = tile
            table_ref[half_table + z * X + tile_at] = swap_halves(tile)

    for (off, part), ref in zip(PARTS, panel_refs):
        place = pl.ds(pl.multiple_of(((x0 + off) & (X - 1)) * QUARTER, QUARTER), QUARTER)
        for y, chip in itertools.product(range(ref.shape[0]), range(CHIPS)):
            panel_ref[(part or 0) * (Y // 2) + y, chip, place, :] = ref[y, chip]
    first_half = lax.broadcasted_iota(jnp.int32, (BLOCK, WIDTH), 1) < BLOCK
    written = []
    for z in range(Z):
        for x in range(X):
            molecule = (z * X + x) * CORES + (core0 ^ core_off)
            left = []
            for y in range(Y):
                k = ((y0 + y) & (Y - 1)) << 1
                one = left_ref[index_ref[k, molecule]]
                two = right_ref[index_ref[k + 1, molecule]]
                left.append(jnp.where(first_half, table_ref[one], table_ref[two]))
            right = [panel_ref[y, z * X + x] for y in range(Y)]
            found = lax.dot_general(
                jnp.concatenate(left, axis=1), jnp.concatenate(right, axis=1), NT,
                preferred_element_type=jnp.float32,
            ).astype(jnp.bfloat16)
            found = jnp.concatenate([found, found], axis=1)
            place = slice((z * X + x) * WIDTH, (z * X + x + 1) * WIDTH)
            if core_off:
                found = jnp.where(first_half == (core0 == 0), before_ref[:, place], found)
            out_ref[:, place] = found
        if core_off:
            place = (slice(None), pl.ds(z * X * WIDTH, X * WIDTH))
            written.append(
                pltpu.make_async_copy(out_ref.at[place], out_hbm.at[place], out_sems.at[z])
            )
            written[-1].start()
    for copy in written:
        copy.wait()


def virtual(core_off, panels, own, virt_index, first_map, *rest):
    shape, table = (BLOCK, BASIS), (MOLECULES, BLOCK, WIDTH)
    scratch = [pltpu.VMEM((Y, CHIPS, BLOCK, WIDTH), jnp.bfloat16)]
    scratch += [pltpu.SMEM((MOLECULES,), jnp.int32)] * 2
    if core_off:
        scratch = [pltpu.VMEM(shape, jnp.bfloat16), *scratch, pltpu.SemaphoreType.DMA((Z,))]
    return call(
        functools.partial(virtual_kernel, core_off),
        [shape] if core_off else [shape, table],
        [SMEM] * 3 + [VMEM] * (len(panels) + len(rest)),
        (ANYWHERE,) if core_off else (VMEM, VMEM),
        scratch,
    )(virt_index.T, first_map, own, *panels, *rest)


def shift(array, axis, by):
    size = SIZES[axis]
    return lax.ppermute(array, axis, [((i + by) % size, i) for i in range(size)])


def ring(array, axis, *between):
    after, before = shift(array, axis, 1), shift(array, axis, -1)
    if between:
        after, before = tie([after, before], *between)
    middle = array.shape[0] // 2
    low, high = shift(before[:middle], axis, -1), shift(after[middle:], axis, 1)
    return [array, after, before, low, high]


def exchange(array):
    return lax.all_to_all(array, ("z", "x"), split_axis=0, concat_axis=0, tiled=True)


def per_device(
    b_tensor, pair_mask, first_map, second_map, occ_blocks, occ_index, virt_blocks, virt_index
):
    own = jnp.stack([lax.axis_index(axis) for axis in SIZES]).astype(jnp.int32)
    both = exchange(spread(own, occ_blocks, virt_blocks))
    occ_plane, virt_quarter = divide(both)
    pieces = [occ_plane] + [shift(occ_plane, "y", by) for by in range(1, Y)]
    rows = ring(mask_rows(pair_mask, b_tensor), "x", occ_plane)
    rows = rows + [shift(part, "core", 1) for part in rows]
    virt_plane = stack([virt_quarter] + [shift(virt_quarter, "y", by) for by in range(1, Y)])
    pieces = pieces + [shift(piece, "core", 1) for piece in pieces]
    half = occupied(dense_panel(pieces, own, occ_index, second_map), rows, own)
    mine = ring(virt_plane, "x", half)
    turned = exchange(*tie([half], *mine[1:3]))
    mine = tie(mine, turned)
    other = [shift(panel, "core", 1) for panel in mine]
    known = (own, virt_index, first_map)
    columns, table = virtual(0, mine, *known, turned)
    return virtual(1, other, *known, table, columns)[0][None]


def solution(mesh):
    shaped = Mesh(mesh.devices.reshape(Z, X, CORES, Y), tuple(SIZES))
    wide = ("z", "x", "core")
    placed = (
        P("y", wide, None),
        P("y", wide, None),
        P(),
        P(),
        P(wide, "y", None, None),
        P(),
        P(wide, "y", None, None),
        P(),
    )
    return jax.shard_map(
        per_device, mesh=shaped, in_specs=placed, out_specs=P("y", wide, None), check_vma=False
    )
```

```python
import functools
import itertools

import jax
import jax.numpy as jnp
from jax import lax
from jax.experimental import pallas as pl
from jax.experimental.pallas import tpu as pltpu
from jax.sharding import Mesh, PartitionSpec as P

Z, X, CORES, Y = 8, 4, 2, 4
SIZES = {"z": Z, "x": X, "core": CORES, "y": Y}
CHIPS = Z * X
BLOCK, WIDTH, QUARTER = 64, 128, 16
MOLECULES = CHIPS * CORES
BASIS = MOLECULES * BLOCK
ANYWHERE = pl.BlockSpec(memory_space=pl.ANY)
SMEM = pl.BlockSpec(memory_space=pltpu.SMEM)
VMEM = pl.BlockSpec(memory_space=pltpu.VMEM)
NT = (((1,), (1,)), ((), ()))


def swap_halves(tile):
    return jnp.concatenate([tile[:, BLOCK:], tile[:, :BLOCK]], axis=1)


def call(kernel, outs, in_specs, out_specs, scratch=(), mib=16):
    return pl.pallas_call(
        kernel,
        out_shape=tuple(jax.ShapeDtypeStruct(shape, jnp.bfloat16) for shape in outs),
        in_specs=in_specs,
        out_specs=out_specs,
        scratch_shapes=list(scratch),
        compiler_params=pltpu.CompilerParams(vmem_limit_bytes=mib * 2**20),
        cost_estimate=pl.CostEstimate(flops=2**10, bytes_accessed=2**10, transcendentals=0),
    )


def mask_kernel(mask_ref, b_ref, masked_ref):
    first_half = lax.broadcasted_iota(jnp.int32, (BLOCK, WIDTH), 1) < BLOCK
    for pair in range(MOLECULES // 2):
        weight = jnp.where(first_half, mask_ref[0, 0, 2 * pair], mask_ref[0, 0, 2 * pair + 1])
        place = slice(pair * WIDTH, (pair + 1) * WIDTH)
        masked_ref[:, place] = b_ref[0, :, place] * weight.astype(jnp.float32).astype(jnp.bfloat16)


def mask_rows(pair_mask, b_tensor):
    return call(mask_kernel, [(BLOCK, BASIS)], [SMEM, VMEM], (VMEM,), mib=8)(pair_mask, b_tensor)[0]


def spread_kernel(own_ref, occ_ref, virt_ref, spread_ref):
    del own_ref
    occ = jnp.concatenate([occ_ref[0, 0], occ_ref[0, 1]], axis=1)
    rows = jnp.concatenate([virt_ref[0, 0], virt_ref[0, 1]], axis=0).astype(jnp.float32)
    virt = rows.T.astype(jnp.bfloat16)
    for z, x in itertools.product(range(Z), range(X)):
        quarter = slice(x * QUARTER, (x + 1) * QUARTER)
        spread_ref[z * X + x, :QUARTER] = occ[quarter]
        spread_ref[z * X + x, QUARTER:] = virt[quarter]


def spread(own, occ_blocks, virt_blocks):
    return call(
        spread_kernel, [(CHIPS, 2 * QUARTER, WIDTH)], [SMEM, VMEM, VMEM], (VMEM,), mib=8
    )(own, occ_blocks, virt_blocks)[0]


def divide_kernel(both_ref, occ_ref, virt_ref):
    for chip in range(CHIPS):
        occ_ref[chip] = both_ref[chip, :QUARTER]
        virt_ref[chip] = both_ref[chip, QUARTER:]


def divide(both):
    return call(
        divide_kernel,
        [(CHIPS, QUARTER, WIDTH)] * 2,
        [VMEM],
        (VMEM, VMEM),
        mib=8,
    )(both)


def stack_kernel(*refs):
    *parts, out_ref = refs
    for y, ref in enumerate(parts):
        out_ref[y] = ref[...]


def stack(parts):
    return call(
        stack_kernel, [(Y, CHIPS, QUARTER, WIDTH)], [VMEM] * Y, (VMEM,), mib=8
    )(*parts)[0]


def tie(arrays, *after):
    count = len(arrays)
    return pl.pallas_call(
        lambda *refs: None,
        out_shape=tuple(jax.ShapeDtypeStruct(array.shape, array.dtype) for array in arrays),
        in_specs=[ANYWHERE] * (count + len(after)),
        out_specs=(ANYWHERE,) * count,
        input_output_aliases={number: number for number in range(count)},
        compiler_params=pltpu.CompilerParams(vmem_limit_bytes=2**20),
    )(*arrays, *after)


PARTS = [(0, None), (1, None), (3, None), (2, 0), (2, 1)]
MEMBERS = 16


def dense_kernel(index_ref, second_ref, own_ref, *refs):
    *piece_refs, dense_ref, piece_ref = refs
    core0, y0 = own_ref[2], own_ref[3]
    for number, ref in enumerate(piece_refs):
        piece_ref[number * CHIPS : (number + 1) * CHIPS] = ref[...]
    side_of = lax.broadcasted_iota(jnp.int32, (QUARTER, WIDTH), 1) // BLOCK
    dense_ref[...] = jnp.zeros_like(dense_ref)
    for chunk in range(0, CHIPS, MEMBERS):
        molecules = [second_ref[(chunk + member) * CORES + core0] for member in range(MEMBERS)]
        places = [(((molecule & 1) ^ core0) << 7) + (molecule >> 1) for molecule in molecules]
        for y_off in range(Y):
            tiles = [piece_ref[place + y_off * CHIPS] for place in places]
            swapped = [swap_halves(tile) for tile in tiles]
            for side in range(2):
                k = (((y0 + y_off) & (Y - 1)) << 1) + side
                placed = []
                for row, molecule in enumerate(molecules, chunk):
                    index = index_ref[k, molecule]
                    place = (
                        pl.ds(row * QUARTER, QUARTER),
                        pl.ds(pl.multiple_of((index >> 1) << 7, WIDTH), WIDTH),
                    )
                    parity = index & 1
                    value = jnp.where(parity == side, tiles[row - chunk], swapped[row - chunk])
                    placed.append((place, jnp.where(side_of == parity, value, dense_ref[place])))
                for place, value in placed:
                    dense_ref[place] = value


def dense_panel(pieces, own, occ_index, second_map):
    shape = (CHIPS * QUARTER, BASIS)
    return call(
        dense_kernel,
        [shape],
        [SMEM] * 3 + [VMEM] * len(pieces),
        (VMEM,),
        [pltpu.VMEM((len(pieces) * CHIPS, QUARTER, WIDTH), jnp.bfloat16)],
        mib=8,
    )(occ_index.T, second_map, own, *pieces)[0]


def occupied_kernel(own_ref, dense_ref, *refs):
    *row_refs, out_ref, rows_ref = refs
    x0, core0 = own_ref[1], own_ref[2]
    for core_off in range(CORES):
        for (off, part), ref in zip(PARTS, row_refs[core_off * len(PARTS) :]):
            block = ((core0 ^ core_off) << 2) + ((x0 + off) & (X - 1))
            place = pl.multiple_of((block << 6) + (part or 0) * (BLOCK // 2), 32)
            rows_ref[pl.ds(place, ref.shape[0]), :] = ref[...]
    product = lax.dot_general(
        dense_ref[...], rows_ref[...], NT, preferred_element_type=jnp.float32
    ).astype(jnp.bfloat16)
    for chip in range(CHIPS):
        out_ref[chip] = product[chip * QUARTER : (chip + 1) * QUARTER]


def occupied(dense, rows, own):
    lanes = CORES * X * BLOCK
    return call(
        occupied_kernel,
        [(CHIPS, QUARTER, lanes)],
        [SMEM] + [VMEM] * (1 + len(rows)),
        (VMEM,),
        [pltpu.VMEM((lanes, BASIS), jnp.bfloat16)],
    )(own, dense, *rows)[0]


def virtual_kernel(core_off, index_ref, first_ref, own_ref, *refs):
    panel_refs, refs = refs[: len(PARTS)], refs[len(PARTS) :]
    if core_off:
        table_ref, before_ref, out_hbm, out_ref, panel_ref, left_ref, right_ref, out_sems = refs
    else:
        rows_ref, out_ref, table_ref, panel_ref, left_ref, right_ref = refs
    x0, core0, y0 = (own_ref[i] for i in range(1, 4))
    half_table = CHIPS * CORES // 2
    for slot in range(MOLECULES):
        z, x, core = slot // (X * CORES), slot // CORES % X, slot % CORES
        place = z * X + core * 2 + x // 2
        molecule = first_ref[slot]
        left_ref[molecule] = place + half_table * (x % 2)
        right_ref[molecule] = place + half_table * (1 - x % 2)
    if not core_off:
        for z, tile_at in itertools.product(range(Z), range(X)):
            lanes = slice(tile_at * WIDTH, (tile_at + 1) * WIDTH)
            tile = jnp.concatenate([rows_ref[z * X + x, :, lanes] for x in range(X)], axis=0)
            table_ref[z * X + tile_at] = tile
            table_ref[half_table + z * X + tile_at] = swap_halves(tile)

    for (off, part), ref in zip(PARTS, panel_refs):
        place = pl.ds(pl.multiple_of(((x0 + off) & (X - 1)) * QUARTER, QUARTER), QUARTER)
        for y, chip in itertools.product(range(ref.shape[0]), range(CHIPS)):
            panel_ref[(part or 0) * (Y // 2) + y, chip, place, :] = ref[y, chip]
    first_half = lax.broadcasted_iota(jnp.int32, (BLOCK, WIDTH), 1) < BLOCK
    written = []
    for z in range(Z):
        for x in range(X):
            molecule = (z * X + x) * CORES + (core0 ^ core_off)
            left = []
            for y in range(Y):
                k = ((y0 + y) & (Y - 1)) << 1
                one = left_ref[index_ref[k, molecule]]
                two = right_ref[index_ref[k + 1, molecule]]
                left.append(jnp.where(first_half, table_ref[one], table_ref[two]))
            right = [panel_ref[y, z * X + x] for y in range(Y)]
            found = lax.dot_general(
                jnp.concatenate(left, axis=1), jnp.concatenate(right, axis=1), NT,
                preferred_element_type=jnp.float32,
            ).astype(jnp.bfloat16)
            found = jnp.concatenate([found, found], axis=1)
            place = slice((z * X + x) * WIDTH, (z * X + x + 1) * WIDTH)
            if core_off:
                found = jnp.where(first_half == (core0 == 0), before_ref[:, place], found)
            out_ref[:, place] = found
        if core_off:
            place = (slice(None), pl.ds(z * X * WIDTH, X * WIDTH))
            written.append(
                pltpu.make_async_copy(out_ref.at[place], out_hbm.at[place], out_sems.at[z])
            )
            written[-1].start()
    for copy in written:
        copy.wait()


def virtual(core_off, panels, own, virt_index, first_map, *rest):
    shape, table = (BLOCK, BASIS), (MOLECULES, BLOCK, WIDTH)
    scratch = [pltpu.VMEM((Y, CHIPS, BLOCK, WIDTH), jnp.bfloat16)]
    scratch += [pltpu.SMEM((MOLECULES,), jnp.int32)] * 2
    if core_off:
        scratch = [pltpu.VMEM(shape, jnp.bfloat16), *scratch, pltpu.SemaphoreType.DMA((Z,))]
    return call(
        functools.partial(virtual_kernel, core_off),
        [shape] if core_off else [shape, table],
        [SMEM] * 3 + [VMEM] * (len(panels) + len(rest)),
        (ANYWHERE,) if core_off else (VMEM, VMEM),
        scratch,
    )(virt_index.T, first_map, own, *panels, *rest)


def shift(array, axis, by):
    size = SIZES[axis]
    return lax.ppermute(array, axis, [((i + by) % size, i) for i in range(size)])


def ring(array, axis, *between):
    after, before = shift(array, axis, 1), shift(array, axis, -1)
    if between:
        after, before = tie([after, before], *between)
    middle = array.shape[0] // 2
    low, high = shift(before[:middle], axis, -1), shift(after[middle:], axis, 1)
    return [array, after, before, low, high]


def exchange(array):
    return lax.all_to_all(array, ("z", "x"), split_axis=0, concat_axis=0, tiled=True)


def per_device(
    b_tensor, pair_mask, first_map, second_map, occ_blocks, occ_index, virt_blocks, virt_index
):
    own = jnp.stack([lax.axis_index(axis) for axis in SIZES]).astype(jnp.int32)
    both = exchange(spread(own, occ_blocks, virt_blocks))
    occ_plane, virt_quarter = divide(both)
    sides = [shift(virt_quarter, "y", by) for by in range(1, Y)]
    virt_plane = stack([virt_quarter] + sides)
    rows = ring(mask_rows(pair_mask, b_tensor), "x", virt_quarter)
    rows = rows + [shift(part, "core", 1) for part in rows]
    (occ_plane,) = tie([occ_plane], *sides)
    pieces = [occ_plane] + [shift(occ_plane, "y", by) for by in range(1, Y)]
    pieces = pieces + [shift(piece, "core", 1) for piece in pieces]
    half = occupied(dense_panel(pieces, own, occ_index, second_map), rows, own)
    mine = ring(virt_plane, "x", half)
    turned = exchange(*tie([half], *mine[1:3]))
    mine = tie(mine, turned)
    other = [shift(panel, "core", 1) for panel in mine]
    known = (own, virt_index, first_map)
    columns, table = virtual(0, mine, *known, turned)
    return virtual(1, other, *known, table, columns)[0][None]


def solution(mesh):
    shaped = Mesh(mesh.devices.reshape(Z, X, CORES, Y), tuple(SIZES))
    wide = ("z", "x", "core")
    placed = (
        P("y", wide, None),
        P("y", wide, None),
        P(),
        P(),
        P(wide, "y", None, None),
        P(),
        P(wide, "y", None, None),
        P(),
    )
    return jax.shard_map(
        per_device, mesh=shaped, in_specs=placed, out_specs=P("y", wide, None), check_vma=False
    )
```
